32 devices in a mesh: row: 8 (over z, x), col: 4 (over y, core).
Axes of the slice: x: 2, y: 2, z: 4, core: 2. Of those that a mesh axis runs over, the one named last changes fastest.
Arguments:
- a_blocks: float32 [1024, 6, 4096], P(('row', 'col')), as said below
- columns: int32 [1024, 6], P(('row', 'col')), may hold values from 0 to 1023, as said below
- tentative: float32 [1024, 4096], P(('row', 'col')), may hold values from -0.75 to 0.75
- aggregate: int32 [1024], P(('row', 'col')), may hold values from 0 to 3, as said below
- owner: int32 [128], P(('row', 'col')), may hold values from 0 to 127, as said below
Outputs:
- coarse_op: float32 [128, 20, 4096], P(('row', 'col'))
The draws below stay inside these ranges and needn't reach their ends.
Inputs may be any that keep to these rules, and one draw needn't show every extreme that they name: Column 0 of block row n is n. Other columns of block row n lie among the block rows of n's device (32 a device, devices in the order of row+col); for the first 8 rows of a device they may also lie among the last 8 rows of the device before it, and for the last 8 rows among the first 8 rows of the device after it, and each such rim row of a device with that neighbour has one. Columns may repeat; repeated blocks add. `aggregate`: every device uses every number from 0 to 3. `owner`: A permutation of the coarse rows. The coarse rows of a device (a // 4) go to positions owned (position // 4) by devices of the same index along row, at most one to each device, so each device owns 4. The diagonal entries of the blocks a_blocks[n, 0] lie between 1.5 and 8.5.
All inputs are finite; a program needn't handle non-finite values.
Results may differ from the reference program's by a relative error of at most 0.0003.
Values sent between devices are 32-bit elements; how exact they have to be, the bound alone decides.
No kernel may reach another device: no remote copies, remote signals or barrier semaphores. Data moves between devices by JAX's collectives and lax.ppermute only.
A program may use at most 256 MiB of HBM per device.

```python
import math
import jax
import jax.numpy as jnp
from jax import lax

B = 64
BC = 64
K = 6
G = 4
R = 32
H = 8
NBLK = 1024
NAGG = 128
N_COL = 4


def draw_a_blocks(key, part):
    key_off, key_diag = jax.random.split(key)
    offdiag = jnp.clip(jax.random.normal(key_off, (NBLK, K, B * B), jnp.float32), -4.0, 4.0) / B ** 0.5
    diag_values = jnp.exp(jax.random.uniform(key_diag, (NBLK, B), jnp.float32, math.log(2.0), math.log(8.0)))
    identity = (jnp.arange(B)[:, None] == jnp.arange(B)[None, :]).astype(jnp.float32)
    self_block = (diag_values[:, :, None] * identity[None]).reshape(NBLK, B * B)
    first_column = (jnp.arange(K) == 0).astype(jnp.float32)
    return offdiag + first_column[None, :, None] * self_block[:, None, :]


def draw_columns(key, part):
    key_own, key_low, key_up, key_coin = jax.random.split(key, 4)
    row_ids = jnp.arange(NBLK, dtype=jnp.int32)
    owner_dev = row_ids // R
    position = row_ids % R
    device_count = NBLK // R
    own_cols = owner_dev[:, None] * R + jax.random.randint(key_own, (NBLK, K), 0, R)
    lower_cols = (owner_dev[:, None] - 1) * R + R - H + jax.random.randint(key_low, (NBLK, K), 0, H)
    upper_cols = (owner_dev[:, None] + 1) * R + jax.random.randint(key_up, (NBLK, K), 0, H)
    coin_flip = jax.random.randint(key_coin, (NBLK, K), 0, 2)
    coin_flip = jnp.where(jnp.arange(K)[None, :] == 1, 1, coin_flip)
    use_lower = (position[:, None] < H) & (owner_dev[:, None] > 0) & (coin_flip == 1)
    use_upper = (position[:, None] >= R - H) & (owner_dev[:, None] < device_count - 1) & (coin_flip == 1)
    chosen = jnp.where(use_lower, lower_cols, jnp.where(use_upper, upper_cols, own_cols))
    chosen = jnp.where(jnp.arange(K)[None, :] == 0, row_ids[:, None], chosen)
    return chosen.astype(jnp.int32)


def draw_aggregate(key, part):
    key_perm, key_base = jax.random.split(key)
    device_count = NBLK // R
    orders = jax.vmap(lambda subkey: jax.random.permutation(subkey, R))(jax.random.split(key_perm, device_count))
    base_ids = jax.random.randint(key_base, (device_count, R), 0, G)
    chosen = jnp.where(orders < G, orders, base_ids)
    return chosen.reshape(NBLK).astype(jnp.int32)


def draw_owner(key, part):
    group_count = NAGG // (G * N_COL)
    shifts = jax.vmap(lambda subkey: jax.random.permutation(subkey, N_COL)[:G])(jax.random.split(key, group_count))
    coarse_ids = jnp.arange(NAGG, dtype=jnp.int32)
    anchor = coarse_ids // G
    within = coarse_ids % G
    group_ids = anchor // N_COL
    column_ids = anchor % N_COL
    moved = shifts[group_ids, within]
    return (group_ids * N_COL * G + (column_ids + moved) % N_COL * G + within).astype(jnp.int32)


def shard_levels(key, extent, cuts, smallest, largest):
    def one(dim, shards_of):
        steps = jax.random.uniform(jax.random.fold_in(jax.random.fold_in(key, 6), dim), (shards_of,), jnp.float32, smallest / len(cuts), largest / len(cuts))
        return jnp.repeat(jnp.exp(steps), extent[dim] // shards_of).reshape((-1,) + (1,) * (len(extent) - dim - 1))

    gain = one(*cuts[0])
    for cut in cuts[1:]:
        gain = gain * one(*cut)
    return gain


def gaussian(stream_key, dims, scale, most, shards=(), kind=jnp.bfloat16):
    array = jax.random.normal(stream_key, dims, jnp.float32) * scale
    if len(shards) > 0:
        array = shard_levels(stream_key, dims, shards, -0.22, 0.18) * array
    return jnp.clip(array, min=-most, max=most).astype(kind)


def setup_inputs(seed: int = 0) -> dict:
    key_list = jax.random.split(jax.random.key(seed), 6)
    return {
        "a_blocks": draw_a_blocks(jax.random.fold_in(key_list[5], 71), 0),
        "columns": draw_columns(jax.random.fold_in(key_list[5], 71), 0),
        "tentative": gaussian(key_list[2], (NBLK, B * BC), B ** -0.5, 0.75, ((0, 32),), jnp.float32),
        "aggregate": draw_aggregate(jax.random.fold_in(key_list[5], 71), 0),
        "owner": draw_owner(jax.random.fold_in(key_list[5], 71), 0),
    }


highest = lax.Precision.HIGHEST
relaxation = 2.0 / 3.0


def prolong_rows(a_rows, col_rows, own_basis, ext_basis, ext_agg, device):
    row_count = col_rows.shape[0]
    local_index = (col_rows - device * R + H).astype(jnp.int32)
    dev_offset = (local_index >= H).astype(jnp.int32) + (local_index >= R + H).astype(jnp.int32)
    labels = (dev_offset * G + jnp.take(ext_agg, local_index)).astype(jnp.int32)
    a_mats = a_rows.reshape(row_count, K, B, B)
    basis_rows = jnp.take(ext_basis, local_index, axis=0).reshape(row_count, K, B, BC)
    applied = jnp.einsum("ikqp,ikpv->ikqv", a_mats, basis_rows, precision=highest)
    diagonal = jnp.diagonal(a_mats[:, 0], axis1=1, axis2=2)
    first_column = (jnp.arange(K) == 0).astype(applied.dtype)
    smooth = first_column[None, :, None, None] * own_basis.reshape(row_count, 1, B, BC) - relaxation * applied / diagonal[:, None, :, None]
    return smooth.reshape(row_count, K, B * BC), labels


def apply_rows(a_group, index_group, ext_smooth, ext_labels):
    count = index_group.shape[0]
    gathered = jnp.take(ext_smooth, index_group, axis=0).reshape(count, K, K, B, BC)
    near_labels = jnp.take(ext_labels, index_group, axis=0)
    onehot = (near_labels[..., None] == jnp.arange(3 * G, dtype=jnp.int32)).astype(gathered.dtype)
    products = jnp.einsum("skqp,skmpw->skmqw", a_group.reshape(count, K, B, B), gathered, precision=highest)
    return jnp.einsum("skmc,skmqw->scqw", onehot, products, precision=highest)


def coarse_part(smooth, labels, applied_rows):
    count = labels.shape[0]
    onehot = (labels[..., None] == jnp.arange(3 * G, dtype=jnp.int32)).astype(smooth.dtype)
    dense = jnp.einsum("ikl,ikqv->ilqv", onehot, smooth.reshape(count, K, B, BC), precision=highest)
    return jnp.einsum("ilqv,icqw->lcvw", dense, applied_rows, precision=highest)


def reference(a_blocks, columns, tentative, aggregate, owner):
    device_count = NBLK // R
    pad_basis = jnp.pad(tentative, ((H, H), (0, 0)))
    pad_agg = jnp.pad(aggregate, (H, H))
    devices = jnp.arange(device_count, dtype=jnp.int32)

    def prolong(device):
        start_row = device * R
        ext_basis = lax.dynamic_slice_in_dim(pad_basis, start_row, R + 2 * H, 0)
        ext_agg = lax.dynamic_slice_in_dim(pad_agg, start_row, R + 2 * H, 0)
        a_rows = lax.dynamic_slice_in_dim(a_blocks, start_row, R, 0)
        col_rows = lax.dynamic_slice_in_dim(columns, start_row, R, 0)
        own_basis = lax.dynamic_slice_in_dim(tentative, start_row, R, 0)
        return prolong_rows(a_rows, col_rows, own_basis, ext_basis, ext_agg, device)

    smooth_all, labels_all = lax.map(prolong, devices)
    smooth_pad = jnp.pad(smooth_all, ((1, 1), (0, 0), (0, 0), (0, 0)))
    labels_pad = jnp.pad(labels_all, ((1, 1), (0, 0), (0, 0)))

    def assemble(device):
        start_row = device * R
        own_rows = lax.dynamic_index_in_dim(smooth_all, device, 0, False)
        own_labels = lax.dynamic_index_in_dim(labels_all, device, 0, False)
        lower_rows = lax.dynamic_index_in_dim(smooth_pad, device, 0, False)[R - H:]
        upper_rows = lax.dynamic_index_in_dim(smooth_pad, device + 2, 0, False)[:H]
        lower_labels = lax.dynamic_index_in_dim(labels_pad, device, 0, False)[R - H:] - G
        upper_labels = lax.dynamic_index_in_dim(labels_pad, device + 2, 0, False)[:H] + G
        ext_smooth = jnp.concatenate([lower_rows, own_rows, upper_rows], axis=0)
        ext_labels = jnp.concatenate([lower_labels, own_labels, upper_labels], axis=0).astype(jnp.int32)
        a_rows = lax.dynamic_slice_in_dim(a_blocks, start_row, R, 0)
        col_rows = lax.dynamic_slice_in_dim(columns, start_row, R, 0)
        local_index = (col_rows - start_row + H).astype(jnp.int32)
        applied_rows = apply_rows(a_rows, local_index, ext_smooth, ext_labels)
        return coarse_part(own_rows, own_labels, applied_rows)

    parts = lax.map(assemble, devices)
    parts_pad = jnp.pad(parts, ((1, 1), (0, 0), (0, 0), (0, 0), (0, 0)))
    own_part = parts[:, G:2 * G]
    from_lower = parts_pad[:-2, 2 * G:]
    from_upper = parts_pad[2:, :G]
    rows_full = jnp.pad(own_part, ((0, 0), (0, 0), (G, G), (0, 0), (0, 0)))
    rows_full = rows_full + jnp.pad(from_lower, ((0, 0), (0, 0), (0, 2 * G), (0, 0), (0, 0)))
    rows_full = rows_full + jnp.pad(from_upper, ((0, 0), (0, 0), (2 * G, 0), (0, 0), (0, 0)))
    coarse_rows = rows_full.reshape(NAGG, 5 * G, BC * BC)
    return jnp.zeros_like(coarse_rows).at[owner].set(coarse_rows)
```

```python
import jax
import jax.numpy as jnp
from jax import lax
from jax.experimental import pallas as pl
from jax.experimental.pallas import tpu as pltpu
from jax.sharding import PartitionSpec as P

B = 64
K = 6
G = 4
R = 32
H = 8
T = 32
E = R + H
SIDE = 2 * H
AXES = ("row", "col")
RELAX = 2.0 / 3.0
F32 = jnp.float32
BF16 = jnp.bfloat16
I32 = jnp.int32


def split(x):
    hi = x.astype(BF16)
    return hi, (x - hi.astype(F32)).astype(BF16)


def lanes_of(shape):
    return lax.broadcasted_iota(I32, shape, 1)


def take_lanes(x, index):
    return jnp.take_along_axis(x, index, axis=1)


def twice(x):
    return jnp.concatenate([x, x], axis=0)


def raw_block(ref, base, row):
    return ref[pl.ds(base + row, T, stride=H), :]


def galerkin_kernel(
    ints, a_own, t_own, a_low, t_low, t_high, *refs, ncol
):
    n_out = 3 * ncol
    outs, (tf, tb, lhs, pf, w, pt_hi, pt_lo, ap, ap_hi, ap_lo, part) = refs[:n_out], refs[n_out:]
    ups, owns, downs = outs[:ncol], outs[ncol : 2 * ncol], outs[2 * ncol :]
    device = ints[9, 4]
    col = lax.rem(device, ncol)

    lane = lanes_of((T, 128))
    half = lax.rem(lane, 64)
    plain = (half, half + 64)
    sorted_half = jnp.where(half < 32, 2 * half, 2 * half - 63)
    sorted_lanes = (sorted_half, sorted_half + 64)

    def doubled(x, index):
        return jnp.concatenate([take_lanes(x, index[0]), take_lanes(x, index[1])], axis=0)

    def load_t(ref, base, row, slot):
        x = doubled(raw_block(ref, base, row), plain)
        hi, lo = split(x)
        tf[slot] = x
        tb[slot] = jnp.concatenate([hi, lo], axis=0)

    def t_rows(i, carry):
        base = (i // H) * (T * H)
        row = lax.rem(i, H)
        load_t(t_low, base, row, i)
        load_t(t_own, base, row, R + i)
        return carry

    lax.fori_loop(0, R, t_rows, 0, unroll=2)

    def t_next(i, carry):
        load_t(t_high, 0, i, 2 * R + i)
        return carry

    lax.fori_loop(0, H, t_next, 0, unroll=2)

    row_of = lax.broadcasted_iota(I32, (64, 128), 0)
    lane_of = lanes_of((64, 128))
    diagonal_mask = row_of == lane_of
    upper_half = lane_of // 64

    def position(column):
        return jnp.clip(column - (device - 1) * R, 0, 2 * R + H - 1)

    def aggregate_of(j):
        block = j // R
        return ints[8 * block, j - R * block]

    def prolong(e, a_ref, base_of, row, columns):
        for pair in range(4):
            pf[e, pair] = jnp.zeros((64, 128), F32)
        scale = None
        for k in range(K):
            x = doubled(raw_block(a_ref, base_of(k), row), sorted_lanes)
            hi, lo = split(x)
            left = jnp.concatenate([hi, lo], axis=1)
            lhs[e * K + k] = left
            j = position(columns(k))
            right = tb[j]
            product = jnp.dot(left, twice(right), preferred_element_type=F32)
            if k == 0:
                diagonal = jnp.sum(jnp.where(diagonal_mask, x, 0.0), axis=1, keepdims=True)
                scale = -RELAX / jnp.where(diagonal == 0.0, 1.0, diagonal)
            value = product * scale
            if k == 0:
                value = value + tf[j]
            slot = aggregate_of(j) + jnp.where(j // R == 1, 0, G)
            pf[e, slot // 2] += jnp.where(upper_half == lax.rem(slot, 2), value, 0.0)

    def prolong_low(i, carry):
        prolong(i, a_low, lambda k: k * (T * H), i, lambda k: ints[2 + k, R - H + i])
        return carry

    def prolong_own(i, carry):
        g = i // H
        prolong(
            H + i,
            a_own,
            lambda k: (k * (R // H) + g) * (T * H),
            lax.rem(i, H),
            lambda k: ints[10 + k, i],
        )
        return carry

    lax.fori_loop(0, H, prolong_low, 0, unroll=2)
    lax.fori_loop(0, R, prolong_own, 0, unroll=2)

    w[E] = jnp.zeros((128, 512), BF16)

    def arrange(i, carry):
        for half_index in range(2):
            e = 2 * i + half_index
            for pair in range(4):
                hi, lo = split(pf[e, pair])
                w[e, 0:64, pair * 128 : pair * 128 + 128] = hi
                w[e, 64:128, pair * 128 : pair * 128 + 128] = lo
        where = pl.ds(pl.multiple_of(i * 128, 128), 128)
        for pair in range(4):
            both = jnp.concatenate([pf[2 * i, pair], pf[2 * i + 1, pair]], axis=0)
            hi, lo = split(both.T)
            pt_hi[pair * 128 : pair * 128 + 128, where] = hi
            pt_lo[pair * 128 : pair * 128 + 128, where] = lo
        return carry

    lax.fori_loop(0, E // 2, arrange, 0)

    def apply(e, columns, lowest):
        ap[0] = jnp.zeros((64, 256), F32)
        ap[2] = jnp.zeros((64, 256), F32)
        own = jnp.zeros((64, 256), F32)
        for k in range(K):
            j = position(columns(k))
            valid = (j >= lowest) & (j < 2 * R)
            source = jnp.where(valid, j - (R - H), E)
            product = jnp.dot(lhs[e * K + k], twice(w[source]), preferred_element_type=F32)
            own = own + product[:, :256]
            place = jnp.where(source < SIDE, 0, 2)
            ap[place] += product[:, 256:]
        where = pl.ds(pl.multiple_of(e * 64, 64), 64)
        for third, value in enumerate((ap[0], own, ap[2])):
            hi, lo = split(value)
            ap_hi[where, third * 256 : third * 256 + 256] = hi
            ap_lo[where, third * 256 : third * 256 + 256] = lo

    def apply_low(i, carry):
        apply(i, lambda k: ints[2 + k, R - H + i], R)
        return carry

    def apply_own(i, carry):
        apply(H + i, lambda k: ints[10 + k, i], R - H)
        return carry

    lax.fori_loop(0, H, apply_low, 0, unroll=2)
    lax.fori_loop(0, R, apply_own, 0, unroll=2)

    def coarse(rows, inner):
        return (
            jnp.dot(pt_hi[rows, inner], ap_hi[inner, :], preferred_element_type=F32)
            + jnp.dot(pt_hi[rows, inner], ap_lo[inner, :], preferred_element_type=F32)
            + jnp.dot(pt_lo[rows, inner], ap_hi[inner, :], preferred_element_type=F32)
        )

    products = (
        coarse(slice(256, 512), slice(0, SIDE * 64)),
        coarse(slice(0, 256), slice(0, E * 64)),
        coarse(slice(256, 512), slice((E - H) * 64, E * 64)),
    )
    for which in range(3):
        for pair in range(6):
            part[which, pair] = products[which][:, pair * 128 : pair * 128 + 128]

    low_lanes = lane < 64

    def give(out, which, s, home, ints_row):
        chosen = jnp.int32(0)
        place = jnp.int32(-1)
        for g in range(G):
            spot = ints[ints_row, g]
            distance = lax.rem(lax.rem(spot // G, ncol) - home + ncol, ncol)
            hit = distance == s
            chosen = jnp.where(hit, g, chosen)
            place = jnp.where(hit, lax.rem(spot, G), place)
        for pair in range(6):
            even = part[which, pair, pl.ds(chosen * 64, T, stride=2), :]
            odd = part[which, pair, pl.ds(chosen * 64 + 1, T, stride=2), :]
            first = jnp.where(low_lanes, even, pltpu.roll(odd, 64, 1))
            second = jnp.where(low_lanes, pltpu.roll(even, 64, 1), odd)
            out[2 * pair * T : (2 * pair + 1) * T, :] = first
            out[(2 * pair + 1) * T : (2 * pair + 2) * T, :] = second
        out[3 * G * T : 3 * G * T + 8, :] = jnp.full((8, 128), place.astype(F32))

    for s in range(ncol):
        give(downs[s], 0, s, lax.rem(col + ncol - 1, ncol), 1)
        give(owns[s], 1, s, col, 9)
        give(ups[s], 2, s, lax.rem(col + 1, ncol), 17)


def combine_kernel(*refs, ncol):
    ups, owns, downs, out = refs[:ncol], refs[ncol : 2 * ncol], refs[2 * ncol : 3 * ncol], refs[-1]
    span = G * T
    for j in range(G):
        for c in range(5):
            value = jnp.zeros((span, 128), F32)
            for s in range(ncol):
                term = None
                for source, shift in ((ups[s], 0), (owns[s], 1), (downs[s], 2)):
                    if 0 <= c - shift < 3:
                        piece = source[(c - shift) * span : (c - shift + 1) * span, :]
                        term = piece if term is None else term + piece
                mark = owns[s][3 * span : 3 * span + 1, :] == float(j)
                value = jnp.where(mark, term, value)
            out[pl.ds(c * span * G + j, span, stride=G), :] = value


def local(a_blocks, columns, tentative, aggregate, owner, *, nrow, ncol):
    count = nrow * ncol
    device = lax.axis_index(AXES).astype(I32)
    up = [(d, d + 1) for d in range(count - 1)]
    down = [(d + 1, d) for d in range(count - 1)]

    a_rows = (
        a_blocks.transpose(1, 0, 2)
        .reshape(K, R // H, H, T, 128)
        .transpose(0, 1, 3, 2, 4)
    )
    t_rows = tentative.reshape(R // H, H, T, 128).transpose(0, 2, 1, 3)
    own_ints = jnp.concatenate(
        [
            jnp.pad(aggregate.reshape(1, R), ((0, 0), (0, 128 - R))),
            jnp.pad(
                jnp.concatenate([owner, device.reshape(1)]).reshape(1, G + 1),
                ((0, 0), (0, 128 - G - 1)),
            ),
            jnp.pad(columns.T, ((0, 0), (0, 128 - R))),
        ],
        axis=0,
    )
    meta = own_ints.astype(F32)
    last = t_rows[R // H - 1].reshape(T * H, 128)
    first = t_rows[0].reshape(T * H, 128)
    small_up = lax.ppermute(jnp.concatenate([last, meta], axis=0), AXES, up)
    small_down = lax.ppermute(jnp.concatenate([first, meta], axis=0), AXES, down)
    big = lax.ppermute(
        jnp.concatenate(
            [
                a_rows[:, R // H - 1].reshape(K * T * H, 128),
                t_rows[: R // H - 1].reshape((R // H - 1) * T * H, 128),
            ],
            axis=0,
        ),
        AXES,
        up,
    )
    ints = jnp.concatenate(
        [small_up[T * H :].astype(I32), own_ints, small_down[T * H :].astype(I32)], axis=0
    )
    t_low = jnp.concatenate([big[K * T * H :], small_up[: T * H]], axis=0)

    payload = jax.ShapeDtypeStruct((3 * G * T + 8, 128), F32)
    vmem = pl.BlockSpec(memory_space=pltpu.VMEM)
    smem = pl.BlockSpec(memory_space=pltpu.SMEM)
    parts = pl.pallas_call(
        lambda *refs: galerkin_kernel(*refs, ncol=ncol),
        out_shape=[payload] * (3 * ncol),
        in_specs=[smem] + [vmem] * 5,
        out_specs=[vmem] * (3 * ncol),
        scratch_shapes=[
            pltpu.VMEM((2 * R + H, 64, 128), F32),
            pltpu.VMEM((2 * R + H, 128, 128), BF16),
            pltpu.VMEM((E * K, 64, 256), BF16),
            pltpu.VMEM((E, 4, 64, 128), F32),
            pltpu.VMEM((E + 1, 128, 512), BF16),
            pltpu.VMEM((512, E * 64), BF16),
            pltpu.VMEM((512, E * 64), BF16),
            pltpu.VMEM((3, 64, 256), F32),
            pltpu.VMEM((E * 64, 768), BF16),
            pltpu.VMEM((E * 64, 768), BF16),
            pltpu.VMEM((3, 6, 256, 128), F32),
        ],
        compiler_params=pltpu.CompilerParams(vmem_limit_bytes=58 * 1024 * 1024),
    )(
        ints,
        a_rows.reshape(K * R * T, 128),
        t_rows.reshape(R * T, 128),
        big[: K * T * H],
        t_low,
        small_down[: T * H],
    )
    ups, owns, downs = parts[:ncol], parts[ncol : 2 * ncol], parts[2 * ncol :]

    def routed(block, offset, s):
        route = []
        for d in range(count):
            home = d + offset
            if 0 <= home < count:
                route.append((d, home // ncol * ncol + (home + s) % ncol))
        if all(source == target for source, target in route):
            return block
        return lax.ppermute(block, AXES, route)

    ups = [routed(ups[s], 1, s) for s in range(ncol)]
    owns = [routed(owns[s], 0, s) for s in range(ncol)]
    downs = [routed(downs[s], -1, s) for s in range(ncol)]
    result = pl.pallas_call(
        lambda *refs: combine_kernel(*refs, ncol=ncol),
        out_shape=jax.ShapeDtypeStruct((5 * G * T * G, 128), F32),
        in_specs=[vmem] * (3 * ncol),
        out_specs=vmem,
        compiler_params=pltpu.CompilerParams(vmem_limit_bytes=32 * 1024 * 1024),
    )(*ups, *owns, *downs)
    return result.reshape(5 * G, T, G, 128).transpose(2, 0, 1, 3).reshape(G, 5 * G, T * 128)


def solution(mesh):
    placed = (
        P(AXES, None, None),
        P(AXES, None),
        P(AXES, None),
        P(AXES),
        P(AXES),
    )
    nrow, ncol = mesh.shape["row"], mesh.shape["col"]
    return jax.shard_map(
        lambda *args: local(*args, nrow=nrow, ncol=ncol),
        mesh=mesh,
        in_specs=placed,
        out_specs=P(AXES, None, None),
        check_vma=False,
    )
```

```python
import jax
import jax.numpy as jnp
from jax import lax
from jax.experimental import pallas as pl
from jax.experimental.pallas import tpu as pltpu
from jax.sharding import PartitionSpec as P

B = 64
K = 6
G = 4
R = 32
H = 8
T = 32
TH = T * H
QUAD = 4
UNROLL = 4
AXES = ("row", "col")
RELAX = 2.0 / 3.0
F32 = jnp.float32
BF16 = jnp.bfloat16
I32 = jnp.int32
MB = 1024 * 1024


def most_batches(rows, columns, ranges):
    return (rows * K + (QUAD - 1) * columns) // QUAD + ranges * (UNROLL - 1) + 1


def split(x):
    hi = x.astype(BF16)
    return hi, (x - hi.astype(F32)).astype(BF16)


def lanes_of(shape):
    return lax.broadcasted_iota(I32, shape, 1)


def raw_block(ref, base, row):
    return ref[pl.ds(base + row, T, stride=H), :]


def doubled(x):
    low = lanes_of((T, 128)) < 64
    other = pltpu.roll(x, 64, 1)
    return jnp.where(low, x, other), jnp.where(low, other, x)


def stacked(x):
    return jnp.concatenate(doubled(x), axis=0)


def right_of(table):
    return jnp.concatenate([table[:64], table[:64], table[64:], table[64:]], axis=0)


def wide(left):
    return jnp.concatenate([left, left], axis=1)


def load_tentative(ref, base, row, tn, tb, slot):
    even, odd = doubled(raw_block(ref, base, row))
    spot = slot & 7
    tn[spot, pl.ds(0, T, stride=2), :] = even
    tn[spot, pl.ds(1, T, stride=2), :] = odd
    hi, lo = split(tn[spot])
    tb[slot] = jnp.concatenate([hi, lo], axis=0)


def prolong(e, a_ref, base_of, row, start, pf, tb, entries, keep):
    row_of = lax.broadcasted_iota(I32, (64, 128), 0)
    row_of = jnp.where(row_of < T, 2 * row_of, 2 * row_of - 63)
    lane_of = lanes_of((64, 128))
    scale = None
    for k in range(K):
        x = stacked(raw_block(a_ref, base_of(k), row))
        rounded = x.astype(BF16).astype(F32)
        left = jnp.where(lane_of < 64, rounded, x - rounded).astype(BF16)
        keep(k, left)
        j, slot = entries(k)
        product = jnp.dot(wide(left), right_of(tb[j]), preferred_element_type=F32)
        if k == 0:
            diagonal = jnp.sum(jnp.where(row_of == lane_of, x, 0.0), axis=1, keepdims=True)
            scale = -RELAX / jnp.where(diagonal == 0.0, 1.0, diagonal)
            for pair in range(4):
                pf[e, pair] = jnp.zeros((64, 128), F32)
            value = product * scale + start
        else:
            value = product * scale
        pf[e, slot >> 1] += jnp.where(lane_of // 64 == (slot & 1), value, 0.0)


def as_right(value, nat, spot, w, e, pair):
    nat[spot, pl.ds(0, T, stride=2), :] = value[:T]
    nat[spot, pl.ds(1, T, stride=2), :] = value[T:]
    hi, lo = split(nat[spot])
    w[e, 0:64, pair * 128 : pair * 128 + 128] = hi
    w[e, 64:128, pair * 128 : pair * 128 + 128] = lo


def as_left(first, second, pt_hi, pt_lo, pair, where):
    hi, lo = split(jnp.concatenate([first, second], axis=0).T)
    pt_hi[pair * 128 : pair * 128 + 128, where] = hi
    pt_lo[pair * 128 : pair * 128 + 128, where] = lo


def place_range(counts, starts, order, batch_source, first, last, begin, dummy):
    def one(source, at):
        starts[source] = at
        after = at + ((counts[source] + QUAD - 1) >> 2)
        for q in range(QUAD):
            order[jnp.maximum(after * QUAD - QUAD, 0) + q] = dummy
        return after

    after = lax.fori_loop(first, last, one, begin)
    for q in range(QUAD * (UNROLL - 1)):
        order[after * QUAD + q] = dummy
    for q in range(UNROLL - 1):
        batch_source[after + q] = first
    return (after + UNROLL - 1) // UNROLL * UNROLL


def fill_order(starts, order, batch_source, rank, pair):
    source = rank >> 9
    spot = starts[source] * QUAD + (rank & 511)
    order[spot] = pair
    batch_source[spot >> 2] = source


def apply_range(order, batch_source, begin, end, lhs, w, w_from, ap, row_from, own, side):
    width = 256 if side is None else 512

    def step(i, carry):
        for u in range(UNROLL):
            b = i * UNROLL + u
            pairs = [order[b * QUAD + q] for q in range(QUAD)]
            left = wide(jnp.concatenate([lhs[pair] for pair in pairs], axis=0))
            right = right_of(w[batch_source[b] - w_from, :, :width])
            product = jnp.dot(left, right, preferred_element_type=F32)
            for q, pair in enumerate(pairs):
                e = row_from(pair >> 3)
                ap[e, own] += product[q * 64 : q * 64 + 64, :256]
                if side is not None:
                    ap[e, side] += product[q * 64 : q * 64 + 64, 256:]
        return carry

    lax.fori_loop(begin // UNROLL, end // UNROLL, step, 0)


def product3(left, right):
    (left_hi, left_lo), (right_hi, right_lo) = left, right
    return (
        jnp.dot(left_hi, right_hi, preferred_element_type=F32)
        + jnp.dot(left_hi, right_lo, preferred_element_type=F32)
        + jnp.dot(left_lo, right_hi, preferred_element_type=F32)
    )


def give(out, part, s, col, ncol, ints, mark):
    chosen = jnp.int32(0)
    place = jnp.int32(-1)
    for g in range(G):
        spot = ints[1, g].astype(I32)
        hit = lax.rem(lax.rem(spot >> 2, ncol) - col + ncol, ncol) == s
        chosen = jnp.where(hit, g, chosen)
        place = jnp.where(hit, spot & 3, place)
    low = lanes_of((T, 128)) < 64
    for pair in range(6):
        even = part[pair, pl.ds(chosen * 64, T, stride=2), :]
        odd = part[pair, pl.ds(chosen * 64 + 1, T, stride=2), :]
        first = jnp.where(low, even, pltpu.roll(odd, 64, 1))
        second = jnp.where(low, pltpu.roll(even, 64, 1), odd)
        out[2 * pair * T : (2 * pair + 1) * T, :] = first
        out[(2 * pair + 1) * T : (2 * pair + 2) * T, :] = second
    if mark:
        out[3 * G * T : 3 * G * T + 8, :] = jnp.full((8, 128), place.astype(F32))


def early_kernel(mine, a_own, t_own, small_up, small_down, *refs, ncol):
    ups, refs = refs[:ncol], refs[ncol:]
    part_out, ap_out, lhs_out, w_out, pt_hi_out, pt_lo_out = refs[:6]
    a_rows, tn, tb, lhs, pf, nat, w, pt_hi_u, pt_lo_u, pt_hi, pt_lo, ap, ap_hi, ap_lo = refs[6:20]
    part_own, part_up = refs[20:22]
    low_ints, high_ints, slots, counts, starts, ranks, order, batch_source, sems = refs[22:]
    copies = [
        pltpu.make_async_copy(a_own, a_rows, sems.at[2]),
        pltpu.make_async_copy(small_up.at[pl.ds(TH, 8)], low_ints, sems.at[0]),
        pltpu.make_async_copy(small_down.at[pl.ds(TH, 8)], high_ints, sems.at[1]),
    ]
    for copy in copies:
        copy.start()

    def t_rows(i, carry):
        load_tentative(t_own, (i // H) * TH, lax.rem(i, H), tn, tb, H + i)
        return carry

    def t_ends(i, carry):
        load_tentative(small_up, 0, i, tn, tb, i)
        load_tentative(small_down, 0, i, tn, tb, R + H + i)
        return carry

    lax.fori_loop(0, R, t_rows, 0, unroll=4)
    lax.fori_loop(0, H, t_ends, 0, unroll=2)
    for copy in copies:
        copy.wait()
    device = mine[1, G].astype(I32)
    col = lax.rem(device, ncol)
    origin = device * R - H
    for i in range(H):
        slots[i] = low_ints[0, R - H + i].astype(I32) + G
        slots[H + R + i] = high_ints[0, i].astype(I32) + G
    for i in range(R):
        slots[H + i] = mine[0, i].astype(I32)
    for i in range(R + 1):
        counts[i] = 0

    lhs[R * 8] = jnp.zeros((64, 128), BF16)

    def prolong_rows(i, carry):
        group = i // H
        row = lax.rem(i, H)

        def entries(k):
            j = mine[2 + k, i].astype(I32) - origin
            source = jnp.where((j >= H) & (j < R + H), j - H, R)
            seen = counts[source]
            counts[source] = seen + 1
            ranks[i * 8 + k] = source * 512 + seen
            return j, slots[j]

        def keep(k, left):
            lhs[i * 8 + k] = left

        start = stacked(raw_block(t_own, group * TH, row))
        prolong(
            i, a_rows, lambda k: (k * (R // H) + group) * TH, row, start, pf, tb, entries, keep
        )
        return carry

    lax.fori_loop(0, R, prolong_rows, 0, unroll=4)

    place = lambda first, last, begin: place_range(
        counts, starts, order, batch_source, first, last, begin, R * 8
    )
    first_end = place(0, H, jnp.int32(0))
    second_end = place(H, R - H, first_end)
    third_end = place(R - H, R, second_end)
    starts[R] = MOST_EARLY

    for third in range(3):
        ap[R, third] = jnp.zeros((64, 256), F32)

    def arrange(i, carry, pairs, w_ref, pt_refs, first):
        for e in (2 * i, 2 * i + 1):
            for pair in range(pairs):
                as_right(pf[e, pair], nat, (e & 1) * 4 + pair, w_ref, e, pair)
            for third in range(3):
                ap[e, third] = jnp.zeros((64, 256), F32)
            for k in range(K):
                fill_order(starts, order, batch_source, ranks[e * 8 + k], e * 8 + k)
        where = pl.ds(pl.multiple_of((i - first // 2) * 128, 128), 128)
        for pair in range(pairs):
            as_left(pf[2 * i, pair], pf[2 * i + 1, pair], *pt_refs, pair, where)
        return carry

    inner = (pt_hi, pt_lo)
    lax.fori_loop(0, H // 2, lambda i, c: arrange(i, c, 4, w, (pt_hi_u, pt_lo_u), 0), 0)
    lax.fori_loop(H // 2, (R - H) // 2, lambda i, c: arrange(i, c, 2, w, inner, H), 0)
    lax.fori_loop((R - H) // 2, R // 2, lambda i, c: arrange(i, c, 4, w, inner, H), 0)

    saved = [
        pltpu.make_async_copy(lhs.at[pl.ds(0, H * 8)], lhs_out, sems.at[3]),
        pltpu.make_async_copy(w.at[pl.ds(0, H)], w_out, sems.at[4]),
        pltpu.make_async_copy(pt_hi_u, pt_hi_out, sems.at[5]),
        pltpu.make_async_copy(pt_lo_u, pt_lo_out, sems.at[6]),
    ]
    for copy in saved:
        copy.start()
    same = lambda e: e
    apply_range(order, batch_source, 0, first_end, lhs, w, 0, ap, same, 1, 0)
    apply_range(order, batch_source, first_end, second_end, lhs, w, 0, ap, same, 1, None)
    apply_range(order, batch_source, second_end, third_end, lhs, w, 0, ap, same, 1, 2)

    saved.append(pltpu.make_async_copy(ap.at[pl.ds(0, H)], ap_out, sems.at[7]))
    saved[-1].start()

    def split_ap(e, carry):
        where = pl.ds(pl.multiple_of((e - H) * 64, 64), 64)
        for third in range(3):
            hi, lo = split(ap[e, third])
            ap_hi[where, third * 256 : third * 256 + 256] = hi
            ap_lo[where, third * 256 : third * 256 + 256] = lo
        return carry

    lax.fori_loop(H, R, split_ap, 0, unroll=2)

    last = slice((R - 2 * H) * 64, (R - H) * 64)
    up = product3(
        (pt_hi[256:512, last], pt_lo[256:512, last]), (ap_hi[last, :], ap_lo[last, :])
    )
    for pair in range(6):
        part_up[pair] = up[:, pair * 128 : pair * 128 + 128]
    for s in range(ncol):
        give(ups[s], part_up, s, col, ncol, high_ints, False)
    own = product3((pt_hi[0:256, :], pt_lo[0:256, :]), (ap_hi[...], ap_lo[...]))
    for pair in range(6):
        part_own[pair] = own[:, pair * 128 : pair * 128 + 128]
    saved.append(pltpu.make_async_copy(part_own, part_out, sems.at[8]))
    saved[-1].start()
    for copy in saved:
        copy.wait()


def late_kernel(mine, small_up, t_first, big, *refs, ncol):
    part_in, ap_in, lhs_in, w_in, pt_hi_in, pt_lo_in = refs[:6]
    owns, downs, refs = refs[6 : 6 + ncol], refs[6 + ncol : 6 + 2 * ncol], refs[6 + 2 * ncol :]
    tn, tb, lhs, pf, nat, w, pt_hi, pt_lo, ap, ap_hi, ap_lo, part_down, part_full = refs[:13]
    t_low, a_low, part_own, ap_u, lhs_u, w_u, pt_hi_u, pt_lo_u = refs[13:21]
    low_ints, slots, counts, starts, ranks, order, batch_source, sems = refs[21:]
    copies = [
        pltpu.make_async_copy(big.at[pl.ds(K * TH, (R - H) * T)], t_low, sems.at[0]),
        pltpu.make_async_copy(small_up.at[pl.ds(TH, 8)], low_ints, sems.at[1]),
        pltpu.make_async_copy(big.at[pl.ds(0, K * TH)], a_low, sems.at[2]),
        pltpu.make_async_copy(lhs_in, lhs_u.at[pl.ds(0, H * 8)], sems.at[3]),
        pltpu.make_async_copy(w_in, w_u, sems.at[4]),
        pltpu.make_async_copy(ap_in, ap_u, sems.at[5]),
        pltpu.make_async_copy(pt_hi_in, pt_hi_u, sems.at[6]),
        pltpu.make_async_copy(pt_lo_in, pt_lo_u, sems.at[7]),
        pltpu.make_async_copy(part_in, part_own, sems.at[8]),
    ]
    for copy in copies:
        copy.start()

    def t_rows(i, carry):
        load_tentative(t_low, (i // H) * TH, lax.rem(i, H), tn, tb, i)
        return carry

    def t_ends(i, carry):
        load_tentative(small_up, 0, i, tn, tb, R - H + i)
        load_tentative(t_first, 0, i, tn, tb, R + i)
        return carry

    lax.fori_loop(0, H, t_ends, 0, unroll=2)
    copies[0].wait()
    lax.fori_loop(0, R - H, t_rows, 0, unroll=4)
    copies[1].wait()
    copies[2].wait()
    device = mine[1, G].astype(I32)
    col = lax.rem(device, ncol)
    origin = (device - 1) * R
    for i in range(R):
        slots[i] = low_ints[0, i].astype(I32) + G
    for i in range(H):
        slots[R + i] = mine[0, i].astype(I32)
    for i in range(2 * H + 1):
        counts[i] = 0

    def rank(valid, j, at):
        source = jnp.where(valid, j - (R - H), 2 * H)
        seen = counts[source]
        counts[source] = seen + 1
        ranks[at] = source * 512 + seen

    def prolong_rows(i, carry):
        def entries(k):
            j = low_ints[2 + k, R - H + i].astype(I32) - origin
            rank(j >= R, j, i * 8 + k)
            return j, slots[j]

        def keep(k, left):
            lhs[i * 8 + k] = left

        for k in range(K):
            j = mine[2 + k, i].astype(I32) - origin
            rank(j < R, j, (H + i) * 8 + k)
        start = stacked(raw_block(small_up, 0, i))
        prolong(i, a_low, lambda k: k * TH, i, start, pf, tb, entries, keep)
        return carry

    lax.fori_loop(0, H, prolong_rows, 0, unroll=4)

    place = lambda first, last, begin: place_range(
        counts, starts, order, batch_source, first, last, begin, H * 8
    )
    first_end = place(0, H, jnp.int32(0))
    second_end = place(H, 2 * H, first_end)
    starts[2 * H] = MOST_LATE
    lhs[H * 8] = jnp.zeros((64, 128), BF16)
    for copy in copies[3:]:
        copy.wait()
    lhs_u[H * 8] = jnp.zeros((64, 128), BF16)
    for side in range(2):
        ap[2 * H, side] = jnp.zeros((64, 256), F32)

    def arrange(i, carry):
        for e in (2 * i, 2 * i + 1):
            for pair in range(4):
                as_right(pf[e, pair], nat, (e & 1) * 4 + pair, w, e, pair)
            for side in range(2):
                ap[e, side] = jnp.zeros((64, 256), F32)
                ap[H + e, side] = ap_u[e, side]
            for k in range(K):
                fill_order(starts, order, batch_source, ranks[e * 8 + k], e * 8 + k)
                fill_order(starts, order, batch_source, ranks[(H + e) * 8 + k], e * 8 + k)
        where = pl.ds(pl.multiple_of(i * 128, 128), 128)
        for pair in range(4):
            as_left(pf[2 * i, pair], pf[2 * i + 1, pair], pt_hi, pt_lo, pair, where)
        return carry

    lax.fori_loop(0, H // 2, arrange, 0)

    apply_range(
        order, batch_source, 0, first_end, lhs_u, w, 0, ap, lambda e: e + H, 1, 0
    )
    apply_range(
        order,
        batch_source,
        first_end,
        second_end,
        lhs,
        w_u,
        H,
        ap,
        lambda e: jnp.where(e == H, 2 * H, e),
        1,
        0,
    )

    def split_ap(e, carry):
        where = pl.ds(pl.multiple_of(e * 64, 64), 64)
        for side in range(2):
            hi, lo = split(ap[e, side])
            ap_hi[where, side * 256 : side * 256 + 256] = hi
            ap_lo[where, side * 256 : side * 256 + 256] = lo
        return carry

    lax.fori_loop(0, 2 * H, split_ap, 0, unroll=2)

    def split_third(e, carry):
        where = pl.ds(pl.multiple_of((H + e) * 64, 64), 64)
        hi, lo = split(ap_u[e, 2])
        ap_hi[where, 512:768] = hi
        ap_lo[where, 512:768] = lo
        return carry

    lax.fori_loop(0, H, split_third, 0, unroll=2)

    lows, highs = slice(0, H * 64), slice(H * 64, 2 * H * 64)

    def coarse(rows):
        high = product3((pt_hi_u[rows, :], pt_lo_u[rows, :]), (ap_hi[highs, :], ap_lo[highs, :]))
        low = product3((pt_hi[rows, :], pt_lo[rows, :]), (ap_hi[lows, :512], ap_lo[lows, :512]))
        return [
            high[:, pair * 128 : pair * 128 + 128]
            + (low[:, pair * 128 : pair * 128 + 128] if pair < 4 else 0.0)
            for pair in range(6)
        ]

    for pair, value in enumerate(coarse(slice(256, 512))):
        part_down[pair] = value
    for s in range(ncol):
        give(downs[s], part_down, s, col, ncol, low_ints, False)
    for pair, value in enumerate(coarse(slice(0, 256))):
        part_full[pair] = value + part_own[pair]
    for s in range(ncol):
        give(owns[s], part_full, s, col, ncol, mine, True)


MOST_EARLY = most_batches(R, R, 3)
MOST_LATE = most_batches(2 * H, 2 * H, 2)


def combine_kernel(mine, *refs, ncol):
    ups, owns, downs = refs[:ncol], refs[ncol : 2 * ncol], refs[2 * ncol : 3 * ncol]
    cross_up, cross_down, out, total = refs[3 * ncol :]
    col = lax.rem(mine[1, G].astype(I32), ncol)
    span = G * T
    for s in range(ncol):
        home = lax.rem(col - s + ncol, ncol)
        total[s, 0 : 4 * span] = jnp.zeros((4 * span, 128), F32)
        total[s, 4 * span : 5 * span] = jnp.zeros((span, 128), F32)
        total[s, span : 4 * span] = owns[s][0 : 3 * span]

        @pl.when(home > 0)
        def _():
            total[s, 0 : 3 * span] += ups[(s + 1) % ncol][...]

        @pl.when(home == 0)
        def _():
            total[s, 0 : 3 * span] += cross_up[...]

        @pl.when(home < ncol - 1)
        def _():
            total[s, 2 * span : 5 * span] += downs[(s - 1) % ncol][...]

        @pl.when(home == ncol - 1)
        def _():
            total[s, 2 * span : 5 * span] += cross_down[...]

    for j in range(G):
        for c in range(5):
            value = jnp.zeros((span, 128), F32)
            for s in range(ncol):
                mark = owns[s][3 * span : 3 * span + 1, :] == float(j)
                value = jnp.where(mark, total[s, c * span : (c + 1) * span], value)
            out[pl.ds(c * span * G + j, span, stride=G), :] = value


def local(a_blocks, columns, tentative, aggregate, owner, *, nrow, ncol):
    count = nrow * ncol
    device = lax.axis_index(AXES).astype(I32)
    col = lax.axis_index("col")
    up = [(d, d + 1) for d in range(count - 1)]
    down = [(d + 1, d) for d in range(count - 1)]

    def lying(blocks):
        shape = blocks.shape
        inner = blocks.reshape(*shape[:-2], shape[-2] // H, H, T, 128)
        return inner.swapaxes(-3, -2).reshape(-1, 128)

    a_own = lying(a_blocks.transpose(1, 0, 2))
    a_last = lying(a_blocks[R - H :].transpose(1, 0, 2))
    t_own = lying(tentative)
    last, first = t_own[(R - H) * T :], t_own[:TH]
    meta = jnp.concatenate(
        [
            jnp.pad(aggregate.reshape(1, R), ((0, 0), (0, 128 - R))),
            jnp.pad(
                jnp.concatenate([owner, device.reshape(1)]).reshape(1, G + 1),
                ((0, 0), (0, 128 - G - 1)),
            ),
            jnp.pad(columns.T, ((0, 0), (0, 128 - R))),
        ],
        axis=0,
    ).astype(F32)
    small_up = lax.ppermute(jnp.concatenate([last, meta], axis=0), AXES, up)
    small_down = lax.ppermute(jnp.concatenate([first, meta], axis=0), AXES, down)
    big = jnp.concatenate([a_last, t_own[: (R - H) * T]], axis=0)
    big, small_up, small_down = lax.optimization_barrier((big, small_up, small_down))
    big = lax.ppermute(big, AXES, up)

    span = 3 * G * T
    plain = jax.ShapeDtypeStruct((span, 128), F32)
    marked = jax.ShapeDtypeStruct((span + 8, 128), F32)
    vmem = pl.BlockSpec(memory_space=pltpu.VMEM)
    smem = pl.BlockSpec(memory_space=pltpu.SMEM)
    hbm = pl.BlockSpec(memory_space=pltpu.HBM)
    state_shapes = [
        pltpu.HBM((6, 256, 128), F32),
        pltpu.HBM((H, 3, 64, 256), F32),
        pltpu.HBM((H * 8, 64, 128), BF16),
        pltpu.HBM((H, 128, 512), BF16),
        pltpu.HBM((512, H * 64), BF16),
        pltpu.HBM((512, H * 64), BF16),
    ]
    outs = pl.pallas_call(
        lambda *refs: early_kernel(*refs, ncol=ncol),
        out_shape=[plain] * ncol + state_shapes,
        in_specs=[smem, hbm] + [vmem] * 3,
        out_specs=[vmem] * ncol + [hbm] * len(state_shapes),
        scratch_shapes=[
            pltpu.VMEM((K * R * T, 128), F32),
            pltpu.VMEM((8, 64, 128), F32),
            pltpu.VMEM((R + 2 * H, 128, 128), BF16),
            pltpu.VMEM((R * 8 + 1, 64, 128), BF16),
            pltpu.VMEM((R, 4, 64, 128), F32),
            pltpu.VMEM((8, 64, 128), F32),
            pltpu.VMEM((R, 128, 512), BF16),
            pltpu.VMEM((512, H * 64), BF16),
            pltpu.VMEM((512, H * 64), BF16),
            pltpu.VMEM((512, (R - H) * 64), BF16),
            pltpu.VMEM((512, (R - H) * 64), BF16),
            pltpu.VMEM((R + 1, 3, 64, 256), F32),
            pltpu.VMEM(((R - H) * 64, 768), BF16),
            pltpu.VMEM(((R - H) * 64, 768), BF16),
            pltpu.VMEM((6, 256, 128), F32),
            pltpu.VMEM((6, 256, 128), F32),
            pltpu.SMEM((8, 128), F32),
            pltpu.SMEM((8, 128), F32),
            pltpu.SMEM((R + 2 * H,), I32),
            pltpu.SMEM((R + 1,), I32),
            pltpu.SMEM((R + 1,), I32),
            pltpu.SMEM((R * 8,), I32),
            pltpu.SMEM((MOST_EARLY * QUAD + R * K,), I32),
            pltpu.SMEM((MOST_EARLY + R * K // QUAD,), I32),
            pltpu.SemaphoreType.DMA((9,)),
        ],
        compiler_params=pltpu.CompilerParams(vmem_limit_bytes=44 * MB),
    )(meta, a_own, t_own, small_up, small_down)
    ups, state = outs[:ncol], [pltpu.with_memory_space_constraint(x, pltpu.HBM) for x in outs[ncol:]]

    def rotated(blocks):
        moved = [blocks[0]]
        for s in range(1, ncol):
            route = [(c, (c + s) % ncol) for c in range(ncol)]
            moved.append(lax.ppermute(blocks[s], "col", route))
        return moved

    def chosen(blocks, index):
        value = blocks[0]
        for s in range(1, ncol):
            value = jnp.where(index == s, blocks[s], value)
        return value

    ups = rotated(ups)
    outs = pl.pallas_call(
        lambda *refs: late_kernel(*refs, ncol=ncol),
        out_shape=[marked] * ncol + [plain] * ncol,
        in_specs=[smem, vmem, vmem, hbm] + [hbm] * len(state_shapes),
        out_specs=[vmem] * (2 * ncol),
        scratch_shapes=[
            pltpu.VMEM((8, 64, 128), F32),
            pltpu.VMEM((R + H, 128, 128), BF16),
            pltpu.VMEM((H * 8 + 1, 64, 128), BF16),
            pltpu.VMEM((H, 4, 64, 128), F32),
            pltpu.VMEM((8, 64, 128), F32),
            pltpu.VMEM((H, 128, 512), BF16),
            pltpu.VMEM((512, H * 64), BF16),
            pltpu.VMEM((512, H * 64), BF16),
            pltpu.VMEM((2 * H + 1, 2, 64, 256), F32),
            pltpu.VMEM((2 * H * 64, 768), BF16),
            pltpu.VMEM((2 * H * 64, 768), BF16),
            pltpu.VMEM((6, 256, 128), F32),
            pltpu.VMEM((6, 256, 128), F32),
            pltpu.VMEM(((R - H) * T, 128), F32),
            pltpu.VMEM((K * TH, 128), F32),
            pltpu.VMEM((6, 256, 128), F32),
            pltpu.VMEM((H, 3, 64, 256), F32),
            pltpu.VMEM((H * 8 + 1, 64, 128), BF16),
            pltpu.VMEM((H, 128, 512), BF16),
            pltpu.VMEM((512, H * 64), BF16),
            pltpu.VMEM((512, H * 64), BF16),
            pltpu.SMEM((8, 128), F32),
            pltpu.SMEM((R + H,), I32),
            pltpu.SMEM((2 * H + 1,), I32),
            pltpu.SMEM((2 * H + 1,), I32),
            pltpu.SMEM((2 * H * 8,), I32),
            pltpu.SMEM((MOST_LATE * QUAD + 2 * H * K,), I32),
            pltpu.SMEM((MOST_LATE + 2 * H * K // QUAD,), I32),
            pltpu.SemaphoreType.DMA((9,)),
        ],
        compiler_params=pltpu.CompilerParams(vmem_limit_bytes=26 * MB),
    )(meta, small_up, first, big, *state)
    owns, downs = outs[:ncol], outs[ncol:]
    downs = rotated(downs)
    owns = rotated(owns)
    cross_up = lax.ppermute(
        chosen(ups, lax.rem(col + 1, ncol)), "row", [(r, r + 1) for r in range(nrow - 1)]
    )
    cross_down = lax.ppermute(
        chosen(downs, col), "row", [(r + 1, r) for r in range(nrow - 1)]
    )
    result = pl.pallas_call(
        lambda *refs: combine_kernel(*refs, ncol=ncol),
        out_shape=jax.ShapeDtypeStruct((5 * G * T * G, 128), F32),
        in_specs=[smem] + [vmem] * (3 * ncol + 2),
        out_specs=vmem,
        scratch_shapes=[pltpu.VMEM((ncol, 5 * G * T, 128), F32)],
        compiler_params=pltpu.CompilerParams(vmem_limit_bytes=16 * MB),
    )(meta, *ups, *owns, *downs, cross_up, cross_down)
    return result.reshape(5 * G, T, G, 128).transpose(2, 0, 1, 3).reshape(G, 5 * G, T * 128)


def solution(mesh):
    placed = (
        P(AXES, None, None),
        P(AXES, None),
        P(AXES, None),
        P(AXES),
        P(AXES),
    )
    nrow, ncol = mesh.shape["row"], mesh.shape["col"]
    return jax.shard_map(
        lambda *args: local(*args, nrow=nrow, ncol=ncol),
        mesh=mesh,
        in_specs=placed,
        out_specs=P(AXES, None, None),
        check_vma=False,
    )
```

```python
import jax
import jax.numpy as jnp
from jax import lax
from jax.experimental import pallas as pl
from jax.experimental.pallas import tpu as pltpu
from jax.sharding import PartitionSpec as P

B = 64
K = 6
G = 4
R = 32
H = 8
T = 32
TH = T * H
QUAD = 4
MANY, FEW = 8, 4
STEP = 8
AXES = ("row", "col")
RELAX = 2.0 / 3.0
F32 = jnp.float32
BF16 = jnp.bfloat16
I32 = jnp.int32
MB = 1024 * 1024


def most_batches(rows, columns, ranges, unroll):
    return (rows * K + (QUAD - 1) * columns) // QUAD + ranges * (unroll - 1) + 1


def split(x):
    hi = x.astype(BF16)
    return hi, (x - hi.astype(F32)).astype(BF16)


def lanes_of(shape):
    return lax.broadcasted_iota(I32, shape, 1)


def raw_block(ref, base, row):
    return ref[pl.ds(base + row, T, stride=H), :]


def doubled(x):
    low = lanes_of((T, 128)) < 64
    other = pltpu.roll(x, 64, 1)
    return jnp.where(low, x, other), jnp.where(low, other, x)


def stacked(x):
    return jnp.concatenate(doubled(x), axis=0)


def right_of(table):
    return jnp.concatenate([table[:64], table[:64], table[64:], table[64:]], axis=0)


def wide(left):
    return jnp.concatenate([left, left], axis=1)


def load_tentative(ref, base, row, tn, tb, slot):
    even, odd = doubled(raw_block(ref, base, row))
    spot = slot & 7
    tn[spot, pl.ds(0, T, stride=2), :] = even
    tn[spot, pl.ds(1, T, stride=2), :] = odd
    hi, lo = split(tn[spot])
    tb[slot] = jnp.concatenate([hi, lo], axis=0)


def prolong(at, a_ref, base_of, row, start, pf, tb, entries, keep):
    row_of = lax.broadcasted_iota(I32, (64, 128), 0)
    row_of = jnp.where(row_of < T, 2 * row_of, 2 * row_of - 63)
    lane_of = lanes_of((64, 128))
    scale = None
    for k in range(K):
        x = stacked(raw_block(a_ref, base_of(k), row))
        rounded = x.astype(BF16).astype(F32)
        left = jnp.where(lane_of < 64, rounded, x - rounded).astype(BF16)
        keep(k, left)
        j, slot = entries(k)
        product = jnp.dot(wide(left), right_of(tb[j]), preferred_element_type=F32)
        if k == 0:
            diagonal = jnp.sum(jnp.where(row_of == lane_of, x, 0.0), axis=1, keepdims=True)
            scale = -RELAX / jnp.where(diagonal == 0.0, 1.0, diagonal)
            for pair in range(4):
                pf[at, pair] = jnp.zeros((64, 128), F32)
            value = product * scale + start
        else:
            value = product * scale
        pf[at, slot >> 1] += jnp.where(lane_of // 64 == (slot & 1), value, 0.0)


def as_right(value, nat, spot, w, e, pair):
    nat[spot, pl.ds(0, T, stride=2), :] = value[:T]
    nat[spot, pl.ds(1, T, stride=2), :] = value[T:]
    hi, lo = split(nat[spot])
    w[e, 0:64, pair * 128 : pair * 128 + 128] = hi
    w[e, 64:128, pair * 128 : pair * 128 + 128] = lo


def as_left(first, second, pt_hi, pt_lo, pair, where):
    hi, lo = split(jnp.concatenate([first, second], axis=0).T)
    pt_hi[pair * 128 : pair * 128 + 128, where] = hi
    pt_lo[pair * 128 : pair * 128 + 128, where] = lo


def place_range(counts, starts, order, batch_source, first, last, begin, dummy, unroll):
    def one(source, at):
        starts[source] = at
        after = at + ((counts[source] + QUAD - 1) >> 2)
        for q in range(QUAD):
            order[jnp.maximum(after * QUAD - QUAD, 0) + q] = dummy
        return after

    after = lax.fori_loop(first, last, one, begin)
    for q in range(QUAD * (unroll - 1)):
        order[after * QUAD + q] = dummy
    for q in range(unroll - 1):
        batch_source[after + q] = first
    return (after + unroll - 1) // unroll * unroll


def fill_order(starts, order, batch_source, rank, pair):
    source = rank >> 9
    spot = starts[source] * QUAD + (rank & 511)
    order[spot] = pair
    batch_source[spot >> 2] = source


def apply_range(order, batch_source, begin, end, lhs, w, w_from, ap, row_from, own, side, unroll):
    width = 256 if side is None else 512

    def step(i, carry):
        for u in range(unroll):
            b = i * unroll + u
            pairs = [order[b * QUAD + q] for q in range(QUAD)]
            left = wide(jnp.concatenate([lhs[pair] for pair in pairs], axis=0))
            right = right_of(w[batch_source[b] - w_from, :, :width])
            product = jnp.dot(left, right, preferred_element_type=F32)
            for q, pair in enumerate(pairs):
                e = row_from(pair >> 3)
                ap[e, own] += product[q * 64 : q * 64 + 64, :256]
                if side is not None:
                    ap[e, side] += product[q * 64 : q * 64 + 64, 256:]
        return carry

    lax.fori_loop(begin // unroll, end // unroll, step, 0)


def product3(left, right):
    (left_hi, left_lo), (right_hi, right_lo) = left, right
    return (
        jnp.dot(left_hi, right_hi, preferred_element_type=F32)
        + jnp.dot(left_hi, right_lo, preferred_element_type=F32)
        + jnp.dot(left_lo, right_hi, preferred_element_type=F32)
    )


def give(out, part, s, col, ncol, ints, mark):
    chosen = jnp.int32(0)
    place = jnp.int32(-1)
    for g in range(G):
        spot = ints[1, g].astype(I32)
        hit = lax.rem(lax.rem(spot >> 2, ncol) - col + ncol, ncol) == s
        chosen = jnp.where(hit, g, chosen)
        place = jnp.where(hit, spot & 3, place)
    low = lanes_of((T, 128)) < 64
    for pair in range(6):
        even = part[pair, pl.ds(chosen * 64, T, stride=2), :]
        odd = part[pair, pl.ds(chosen * 64 + 1, T, stride=2), :]
        first = jnp.where(low, even, pltpu.roll(odd, 64, 1))
        second = jnp.where(low, pltpu.roll(even, 64, 1), odd)
        out[2 * pair * T : (2 * pair + 1) * T, :] = first
        out[(2 * pair + 1) * T : (2 * pair + 2) * T, :] = second
    if mark:
        out[3 * G * T : 3 * G * T + 8, :] = jnp.full((8, 128), place.astype(F32))


def early_kernel(mine, a_own, t_own, small_up, small_down, *refs, ncol):
    ups, refs = refs[:ncol], refs[ncol:]
    part_out, ap_out, lhs_out, w_out, pt_hi_out, pt_lo_out = refs[:6]
    a_rows, tn, tb, lhs, w, pt_hi_u, pt_lo_u, pt_hi, pt_lo, ap, ap_hi, ap_lo = refs[6:18]
    part_own, part_up = refs[18:20]
    pf, nat = refs[20 : 20 + STEP], refs[20 + STEP : 20 + 2 * STEP]
    refs = refs[20 + 2 * STEP :]
    low_ints, high_ints, slots, counts, starts, ranks, order, batch_source, sems = refs
    whole = pltpu.make_async_copy(a_own, a_rows, sems.at[2])
    whole.start()
    copies = [
        pltpu.make_async_copy(small_up.at[pl.ds(TH, 8)], low_ints, sems.at[0]),
        pltpu.make_async_copy(small_down.at[pl.ds(TH, 8)], high_ints, sems.at[1]),
    ]
    for copy in copies:
        copy.start()

    def t_rows(i, carry):
        load_tentative(t_own, (i // H) * TH, lax.rem(i, H), tn, tb, H + i)
        return carry

    def t_ends(i, carry):
        load_tentative(small_up, 0, i, tn, tb, i)
        load_tentative(small_down, 0, i, tn, tb, R + H + i)
        return carry

    lax.fori_loop(0, R, t_rows, 0, unroll=4)
    lax.fori_loop(0, H, t_ends, 0, unroll=2)
    for copy in copies:
        copy.wait()
    device = mine[1, G].astype(I32)
    col = lax.rem(device, ncol)
    origin = device * R - H
    for i in range(H):
        slots[i] = low_ints[0, R - H + i].astype(I32) + G
        slots[H + R + i] = high_ints[0, i].astype(I32) + G
    for i in range(R):
        slots[H + i] = mine[0, i].astype(I32)
    for i in range(R + 1):
        counts[i] = 0

    lhs[R * 8] = jnp.zeros((64, 128), BF16)

    def prolong_row(i, group, u):
        row = i - group * H

        def entries(k):
            j = mine[2 + k, i].astype(I32) - origin
            source = jnp.where((j >= H) & (j < R + H), j - H, R)
            seen = counts[source]
            counts[source] = seen + 1
            ranks[i * 8 + k] = source * 512 + seen
            return j, slots[j]

        def keep(k, left):
            lhs[i * 8 + k] = left

        start = stacked(raw_block(t_own, group * TH, row))
        base_of = lambda k: (k * (R // H) + group) * TH
        prolong(i // STEP, a_rows, base_of, row, start, pf[u], tb, entries, keep)

    whole.wait()

    def prolong_rows(i, carry):
        for u in range(STEP):
            prolong_row(i * STEP + u, i // (H // STEP), u)
        return carry

    lax.fori_loop(0, R // STEP, prolong_rows, 0)

    place = lambda first, last, begin: place_range(
        counts, starts, order, batch_source, first, last, begin, R * 8, MANY
    )
    first_end = place(0, H, jnp.int32(0))
    second_end = place(H, R - H, first_end)
    third_end = place(R - H, R, second_end)
    starts[R] = MOST_EARLY

    for third in range(3):
        ap[R, third] = jnp.zeros((64, 256), F32)

    def arrange(i, carry, pairs, pt_refs, first):
        for u in range(STEP):
            e = i * STEP + u
            for pair in range(pairs):
                as_right(pf[u][i, pair], nat[u], pair, w, e, pair)
            for third in range(3):
                ap[e, third] = jnp.zeros((64, 256), F32)
            for k in range(K):
                fill_order(starts, order, batch_source, ranks[e * 8 + k], e * 8 + k)
        for u in range(0, STEP, 2):
            where = pl.ds(pl.multiple_of((i * STEP + u - first) * 64, 128), 128)
            for pair in range(pairs):
                as_left(pf[u][i, pair], pf[u + 1][i, pair], *pt_refs, pair, where)
        return carry

    inner = (pt_hi, pt_lo)
    at = [0, H // STEP, (R - H) // STEP, R // STEP]
    lax.fori_loop(at[0], at[1], lambda i, c: arrange(i, c, 4, (pt_hi_u, pt_lo_u), 0), 0)
    lax.fori_loop(at[1], at[2], lambda i, c: arrange(i, c, 2, inner, H), 0)
    lax.fori_loop(at[2], at[3], lambda i, c: arrange(i, c, 4, inner, H), 0)

    saved = [
        pltpu.make_async_copy(lhs.at[pl.ds(0, H * 8)], lhs_out, sems.at[3]),
        pltpu.make_async_copy(w.at[pl.ds(0, H)], w_out, sems.at[4]),
        pltpu.make_async_copy(pt_hi_u, pt_hi_out, sems.at[5]),
        pltpu.make_async_copy(pt_lo_u, pt_lo_out, sems.at[6]),
    ]
    for copy in saved:
        copy.start()
    same = lambda e: e
    apply_range(order, batch_source, 0, first_end, lhs, w, 0, ap, same, 1, 0, MANY)
    apply_range(order, batch_source, first_end, second_end, lhs, w, 0, ap, same, 1, None, MANY)
    apply_range(order, batch_source, second_end, third_end, lhs, w, 0, ap, same, 1, 2, MANY)

    saved.append(pltpu.make_async_copy(ap.at[pl.ds(0, H)], ap_out, sems.at[7]))
    saved[-1].start()

    def split_ap(e, carry):
        where = pl.ds(pl.multiple_of((e - H) * 64, 64), 64)
        for third in range(3):
            hi, lo = split(ap[e, third])
            ap_hi[where, third * 256 : third * 256 + 256] = hi
            ap_lo[where, third * 256 : third * 256 + 256] = lo
        return carry

    lax.fori_loop(H, R, split_ap, 0, unroll=2)

    own = product3((pt_hi[0:256, :], pt_lo[0:256, :]), (ap_hi[...], ap_lo[...]))
    for pair in range(6):
        part_own[pair] = own[:, pair * 128 : pair * 128 + 128]
    saved.append(pltpu.make_async_copy(part_own, part_out, sems.at[8]))
    saved[-1].start()
    last = slice((R - 2 * H) * 64, (R - H) * 64)
    up = product3(
        (pt_hi[256:512, last], pt_lo[256:512, last]), (ap_hi[last, :], ap_lo[last, :])
    )
    for pair in range(6):
        part_up[pair] = up[:, pair * 128 : pair * 128 + 128]
    for s in range(ncol):
        give(ups[s], part_up, s, col, ncol, high_ints, False)
    for copy in saved:
        copy.wait()


def late_kernel(mine, small_up, t_first, big, *refs, ncol):
    part_in, ap_in, lhs_in, w_in, pt_hi_in, pt_lo_in = refs[:6]
    owns, downs, refs = refs[6 : 6 + ncol], refs[6 + ncol : 6 + 2 * ncol], refs[6 + 2 * ncol :]
    tn, tb, lhs, w, pt_hi, pt_lo, ap, ap_hi, ap_lo, part_down, part_full = refs[:11]
    t_low, a_low, part_own, ap_u, lhs_u, w_u, pt_hi_u, pt_lo_u = refs[11:19]
    pf, nat = refs[19 : 19 + STEP], refs[19 + STEP : 19 + 2 * STEP]
    low_ints, slots, counts, starts, ranks, order, batch_source, sems = refs[19 + 2 * STEP :]
    copies = [
        pltpu.make_async_copy(big.at[pl.ds(K * TH, (R - H) * T)], t_low, sems.at[0]),
        pltpu.make_async_copy(small_up.at[pl.ds(TH, 8)], low_ints, sems.at[1]),
        pltpu.make_async_copy(big.at[pl.ds(0, K * TH)], a_low, sems.at[2]),
        pltpu.make_async_copy(lhs_in, lhs_u.at[pl.ds(0, H * 8)], sems.at[3]),
        pltpu.make_async_copy(w_in, w_u, sems.at[4]),
        pltpu.make_async_copy(ap_in, ap_u, sems.at[5]),
        pltpu.make_async_copy(pt_hi_in, pt_hi_u, sems.at[6]),
        pltpu.make_async_copy(pt_lo_in, pt_lo_u, sems.at[7]),
        pltpu.make_async_copy(part_in, part_own, sems.at[8]),
    ]
    for copy in copies:
        copy.start()

    def t_rows(i, carry):
        load_tentative(t_low, (i // H) * TH, lax.rem(i, H), tn, tb, i)
        return carry

    def t_ends(i, carry):
        load_tentative(small_up, 0, i, tn, tb, R - H + i)
        load_tentative(t_first, 0, i, tn, tb, R + i)
        return carry

    lax.fori_loop(0, H, t_ends, 0, unroll=2)
    copies[0].wait()
    lax.fori_loop(0, R - H, t_rows, 0, unroll=4)
    copies[1].wait()
    copies[2].wait()
    device = mine[1, G].astype(I32)
    col = lax.rem(device, ncol)
    origin = (device - 1) * R
    for i in range(R):
        slots[i] = low_ints[0, i].astype(I32) + G
    for i in range(H):
        slots[R + i] = mine[0, i].astype(I32)
    for i in range(2 * H + 1):
        counts[i] = 0

    def rank(valid, j, at):
        source = jnp.where(valid, j - (R - H), 2 * H)
        seen = counts[source]
        counts[source] = seen + 1
        ranks[at] = source * 512 + seen

    def prolong_row(i, u):
        def entries(k):
            j = low_ints[2 + k, R - H + i].astype(I32) - origin
            rank(j >= R, j, i * 8 + k)
            return j, slots[j]

        def keep(k, left):
            lhs[i * 8 + k] = left

        for k in range(K):
            j = mine[2 + k, i].astype(I32) - origin
            rank(j < R, j, (H + i) * 8 + k)
        start = stacked(raw_block(small_up, 0, i))
        prolong(i // STEP, a_low, lambda k: k * TH, i, start, pf[u], tb, entries, keep)

    def prolong_rows(i, carry):
        for u in range(STEP):
            prolong_row(i * STEP + u, u)
        return carry

    lax.fori_loop(0, H // STEP, prolong_rows, 0)

    place = lambda first, last, begin: place_range(
        counts, starts, order, batch_source, first, last, begin, H * 8, FEW
    )
    first_end = place(0, H, jnp.int32(0))
    second_end = place(H, 2 * H, first_end)
    starts[2 * H] = MOST_LATE
    lhs[H * 8] = jnp.zeros((64, 128), BF16)
    for copy in copies[3:]:
        copy.wait()
    lhs_u[H * 8] = jnp.zeros((64, 128), BF16)
    for side in range(2):
        ap[2 * H, side] = jnp.zeros((64, 256), F32)

    def arrange(i, carry):
        for u in range(STEP):
            e = i * STEP + u
            for pair in range(4):
                as_right(pf[u][i, pair], nat[u], pair, w, e, pair)
            for side in range(2):
                ap[e, side] = jnp.zeros((64, 256), F32)
                ap[H + e, side] = ap_u[e, side]
            for k in range(K):
                fill_order(starts, order, batch_source, ranks[e * 8 + k], e * 8 + k)
                fill_order(starts, order, batch_source, ranks[(H + e) * 8 + k], e * 8 + k)
        for u in range(0, STEP, 2):
            where = pl.ds(pl.multiple_of((i * STEP + u) * 64, 128), 128)
            for pair in range(4):
                as_left(pf[u][i, pair], pf[u + 1][i, pair], pt_hi, pt_lo, pair, where)
        return carry

    lax.fori_loop(0, H // STEP, arrange, 0)

    apply_range(
        order, batch_source, 0, first_end, lhs_u, w, 0, ap, lambda e: e + H, 1, 0, FEW
    )
    apply_range(
        order,
        batch_source,
        first_end,
        second_end,
        lhs,
        w_u,
        H,
        ap,
        lambda e: jnp.where(e == H, 2 * H, e),
        1,
        0,
        FEW,
    )

    def split_ap(e, carry):
        where = pl.ds(pl.multiple_of(e * 64, 64), 64)
        for side in range(2):
            hi, lo = split(ap[e, side])
            ap_hi[where, side * 256 : side * 256 + 256] = hi
            ap_lo[where, side * 256 : side * 256 + 256] = lo
        return carry

    lax.fori_loop(0, 2 * H, split_ap, 0, unroll=2)

    def split_third(e, carry):
        where = pl.ds(pl.multiple_of((H + e) * 64, 64), 64)
        hi, lo = split(ap_u[e, 2])
        ap_hi[where, 512:768] = hi
        ap_lo[where, 512:768] = lo
        return carry

    lax.fori_loop(0, H, split_third, 0, unroll=2)

    lows, highs = slice(0, H * 64), slice(H * 64, 2 * H * 64)

    def coarse(rows):
        high = product3((pt_hi_u[rows, :], pt_lo_u[rows, :]), (ap_hi[highs, :], ap_lo[highs, :]))
        low = product3((pt_hi[rows, :], pt_lo[rows, :]), (ap_hi[lows, :512], ap_lo[lows, :512]))
        return [
            high[:, pair * 128 : pair * 128 + 128]
            + (low[:, pair * 128 : pair * 128 + 128] if pair < 4 else 0.0)
            for pair in range(6)
        ]

    for pair, value in enumerate(coarse(slice(256, 512))):
        part_down[pair] = value
    for s in range(ncol):
        give(downs[s], part_down, s, col, ncol, low_ints, False)
    for pair, value in enumerate(coarse(slice(0, 256))):
        part_full[pair] = value + part_own[pair]
    for s in range(ncol):
        give(owns[s], part_full, s, col, ncol, mine, True)


MOST_EARLY = most_batches(R, R, 3, MANY)
MOST_LATE = most_batches(2 * H, 2 * H, 2, FEW)


def combine_kernel(mine, *refs, ncol):
    ups, owns, downs = refs[:ncol], refs[ncol : 2 * ncol], refs[2 * ncol : 3 * ncol]
    cross_up, cross_down, out, total = refs[3 * ncol :]
    col = lax.rem(mine[1, G].astype(I32), ncol)
    span = G * T
    for s in range(ncol):
        home = lax.rem(col - s + ncol, ncol)
        total[s, 0:span] = jnp.zeros((span, 128), F32)
        total[s, 4 * span : 5 * span] = jnp.zeros((span, 128), F32)
        total[s, span : 4 * span] = owns[s][0 : 3 * span]

        @pl.when(home > 0)
        def _():
            total[s, 0 : 3 * span] += ups[(s + 1) % ncol][...]

        @pl.when(home == 0)
        def _():
            total[s, 0 : 3 * span] += cross_up[...]

        @pl.when(home < ncol - 1)
        def _():
            total[s, 2 * span : 5 * span] += downs[(s - 1) % ncol][...]

        @pl.when(home == ncol - 1)
        def _():
            total[s, 2 * span : 5 * span] += cross_down[...]

    for j in range(G):
        for c in range(5):
            value = jnp.zeros((span, 128), F32)
            for s in range(ncol):
                mark = owns[s][3 * span : 3 * span + 1, :] == float(j)
                value = jnp.where(mark, total[s, c * span : (c + 1) * span], value)
            out[pl.ds(c * span * G + j, span, stride=G), :] = value


def local(a_blocks, columns, tentative, aggregate, owner, *, nrow, ncol):
    count = nrow * ncol
    device = lax.axis_index(AXES).astype(I32)
    col = lax.axis_index("col")
    up = [(d, d + 1) for d in range(count - 1)]
    down = [(d + 1, d) for d in range(count - 1)]

    def lying(blocks):
        shape = blocks.shape
        inner = blocks.reshape(*shape[:-2], shape[-2] // H, H, T, 128)
        return inner.swapaxes(-3, -2).reshape(-1, 128)

    a_own = lying(a_blocks.transpose(1, 0, 2))
    a_last = lying(a_blocks[R - H :].transpose(1, 0, 2))
    t_own = lying(tentative)
    last, first = t_own[(R - H) * T :], t_own[:TH]
    meta = jnp.concatenate(
        [
            jnp.pad(aggregate.reshape(1, R), ((0, 0), (0, 128 - R))),
            jnp.pad(
                jnp.concatenate([owner, device.reshape(1)]).reshape(1, G + 1),
                ((0, 0), (0, 128 - G - 1)),
            ),
            jnp.pad(columns.T, ((0, 0), (0, 128 - R))),
        ],
        axis=0,
    ).astype(F32)
    small_up = lax.ppermute(jnp.concatenate([last, meta], axis=0), AXES, up)
    small_down = lax.ppermute(jnp.concatenate([first, meta], axis=0), AXES, down)
    big = jnp.concatenate([a_last, t_own[: (R - H) * T]], axis=0)
    big = lax.ppermute(big, AXES, up)

    span = 3 * G * T
    plain = jax.ShapeDtypeStruct((span, 128), F32)
    marked = jax.ShapeDtypeStruct((span + 8, 128), F32)
    vmem = pl.BlockSpec(memory_space=pltpu.VMEM)
    smem = pl.BlockSpec(memory_space=pltpu.SMEM)
    hbm = pl.BlockSpec(memory_space=pltpu.HBM)
    state_shapes = [
        pltpu.HBM((6, 256, 128), F32),
        pltpu.HBM((H, 3, 64, 256), F32),
        pltpu.HBM((H * 8, 64, 128), BF16),
        pltpu.HBM((H, 128, 512), BF16),
        pltpu.HBM((512, H * 64), BF16),
        pltpu.HBM((512, H * 64), BF16),
    ]
    outs = pl.pallas_call(
        lambda *refs: early_kernel(*refs, ncol=ncol),
        out_shape=[plain] * ncol + state_shapes,
        in_specs=[smem, hbm] + [vmem] * 3,
        out_specs=[vmem] * ncol + [hbm] * len(state_shapes),
        scratch_shapes=[
            pltpu.VMEM((K * R * T, 128), F32),
            pltpu.VMEM((8, 64, 128), F32),
            pltpu.VMEM((R + 2 * H, 128, 128), BF16),
            pltpu.VMEM((R * 8 + 1, 64, 128), BF16),
            pltpu.VMEM((R, 128, 512), BF16),
            pltpu.VMEM((512, H * 64), BF16),
            pltpu.VMEM((512, H * 64), BF16),
            pltpu.VMEM((512, (R - H) * 64), BF16),
            pltpu.VMEM((512, (R - H) * 64), BF16),
            pltpu.VMEM((R + 1, 3, 64, 256), F32),
            pltpu.VMEM(((R - H) * 64, 768), BF16),
            pltpu.VMEM(((R - H) * 64, 768), BF16),
            pltpu.VMEM((6, 256, 128), F32),
            pltpu.VMEM((6, 256, 128), F32),
            *[pltpu.VMEM((R // STEP, 4, 64, 128), F32)] * STEP,
            *[pltpu.VMEM((4, 64, 128), F32)] * STEP,
            pltpu.SMEM((8, 128), F32),
            pltpu.SMEM((8, 128), F32),
            pltpu.SMEM((R + 2 * H,), I32),
            pltpu.SMEM((R + 1,), I32),
            pltpu.SMEM((R + 1,), I32),
            pltpu.SMEM((R * 8,), I32),
            pltpu.SMEM((MOST_EARLY * QUAD + R * K,), I32),
            pltpu.SMEM((MOST_EARLY + R * K // QUAD,), I32),
            pltpu.SemaphoreType.DMA((9,)),
        ],
        compiler_params=pltpu.CompilerParams(vmem_limit_bytes=44 * MB),
        cost_estimate=pl.CostEstimate(flops=22 * 10**9, bytes_accessed=12 * MB, transcendentals=0),
    )(meta, a_own, t_own, small_up, small_down)
    ups, state = outs[:ncol], [pltpu.with_memory_space_constraint(x, pltpu.HBM) for x in outs[ncol:]]

    def rotated(blocks):
        moved = [blocks[0]]
        for s in range(1, ncol):
            route = [(c, (c + s) % ncol) for c in range(ncol)]
            moved.append(lax.ppermute(blocks[s], "col", route))
        return moved

    def chosen(blocks, index):
        value = blocks[0]
        for s in range(1, ncol):
            value = jnp.where(index == s, blocks[s], value)
        return value

    ups = rotated(ups)
    outs = pl.pallas_call(
        lambda *refs: late_kernel(*refs, ncol=ncol),
        out_shape=[marked] * ncol + [plain] * ncol,
        in_specs=[smem, vmem, vmem, hbm] + [hbm] * len(state_shapes),
        out_specs=[vmem] * (2 * ncol),
        scratch_shapes=[
            pltpu.VMEM((8, 64, 128), F32),
            pltpu.VMEM((R + H, 128, 128), BF16),
            pltpu.VMEM((H * 8 + 1, 64, 128), BF16),
            pltpu.VMEM((H, 128, 512), BF16),
            pltpu.VMEM((512, H * 64), BF16),
            pltpu.VMEM((512, H * 64), BF16),
            pltpu.VMEM((2 * H + 1, 2, 64, 256), F32),
            pltpu.VMEM((2 * H * 64, 768), BF16),
            pltpu.VMEM((2 * H * 64, 768), BF16),
            pltpu.VMEM((6, 256, 128), F32),
            pltpu.VMEM((6, 256, 128), F32),
            pltpu.VMEM(((R - H) * T, 128), F32),
            pltpu.VMEM((K * TH, 128), F32),
            pltpu.VMEM((6, 256, 128), F32),
            pltpu.VMEM((H, 3, 64, 256), F32),
            pltpu.VMEM((H * 8 + 1, 64, 128), BF16),
            pltpu.VMEM((H, 128, 512), BF16),
            pltpu.VMEM((512, H * 64), BF16),
            pltpu.VMEM((512, H * 64), BF16),
            *[pltpu.VMEM((H // STEP, 4, 64, 128), F32)] * STEP,
            *[pltpu.VMEM((4, 64, 128), F32)] * STEP,
            pltpu.SMEM((8, 128), F32),
            pltpu.SMEM((R + H,), I32),
            pltpu.SMEM((2 * H + 1,), I32),
            pltpu.SMEM((2 * H + 1,), I32),
            pltpu.SMEM((2 * H * 8,), I32),
            pltpu.SMEM((MOST_LATE * QUAD + 2 * H * K,), I32),
            pltpu.SMEM((MOST_LATE + 2 * H * K // QUAD,), I32),
            pltpu.SemaphoreType.DMA((9,)),
        ],
        compiler_params=pltpu.CompilerParams(vmem_limit_bytes=26 * MB),
    )(meta, small_up, first, big, *state)
    owns, downs = outs[:ncol], outs[ncol:]
    downs = rotated(downs)
    to_next = chosen(ups, lax.rem(col + 1, ncol))
    to_last = chosen(downs, col)
    to_next, downs[0] = lax.optimization_barrier((to_next, downs[0]))
    cross_up = lax.ppermute(to_next, "row", [(r, r + 1) for r in range(nrow - 1)])
    cross_down = lax.ppermute(to_last, "row", [(r + 1, r) for r in range(nrow - 1)])
    owns = rotated(owns)
    result = pl.pallas_call(
        lambda *refs: combine_kernel(*refs, ncol=ncol),
        out_shape=jax.ShapeDtypeStruct((5 * G * T * G, 128), F32),
        in_specs=[smem] + [vmem] * (3 * ncol + 2),
        out_specs=vmem,
        scratch_shapes=[pltpu.VMEM((ncol, 5 * G * T, 128), F32)],
        compiler_params=pltpu.CompilerParams(vmem_limit_bytes=16 * MB),
    )(meta, *ups, *owns, *downs, cross_up, cross_down)
    return result.reshape(5 * G, T, G, 128).transpose(2, 0, 1, 3).reshape(G, 5 * G, T * 128)


def solution(mesh):
    placed = (
        P(AXES, None, None),
        P(AXES, None),
        P(AXES, None),
        P(AXES),
        P(AXES),
    )
    nrow, ncol = mesh.shape["row"], mesh.shape["col"]
    return jax.shard_map(
        lambda *args: local(*args, nrow=nrow, ncol=ncol),
        mesh=mesh,
        in_specs=placed,
        out_specs=P(AXES, None, None),
        check_vma=False,
    )
```

```python
import jax
import jax.numpy as jnp
from jax import lax
from jax.experimental import pallas as pl
from jax.experimental.pallas import tpu as pltpu
from jax.sharding import PartitionSpec as P

B = 64
K = 6
G = 4
R = 32
H = 8
T = 32
TH = T * H
QUAD = 4
MANY, FEW = 8, 12
STEP = 8
AXES = ("row", "col")
RELAX = 2.0 / 3.0
F32 = jnp.float32
BF16 = jnp.bfloat16
I32 = jnp.int32
MB = 1024 * 1024


def most_batches(rows, columns, ranges, unroll):
    return (rows * K + (QUAD - 1) * columns) // QUAD + ranges * (unroll - 1) + 1


def split(x):
    hi = x.astype(BF16)
    return hi, (x - hi.astype(F32)).astype(BF16)


def lanes_of(shape):
    return lax.broadcasted_iota(I32, shape, 1)


def raw_block(ref, base, row):
    return ref[pl.ds(base + row, T, stride=H), :]


def doubled(x):
    low = lanes_of((T, 128)) < 64
    other = pltpu.roll(x, 64, 1)
    return jnp.where(low, x, other), jnp.where(low, other, x)


def stacked(x):
    return jnp.concatenate(doubled(x), axis=0)


def right_of(table):
    return jnp.concatenate([table[:64], table[:64], table[64:], table[64:]], axis=0)


def wide(left):
    return jnp.concatenate([left, left], axis=1)


def load_tentative(ref, base, row, tn, tb, slot):
    even, odd = doubled(raw_block(ref, base, row))
    spot = slot & 7
    tn[spot, pl.ds(0, T, stride=2), :] = even
    tn[spot, pl.ds(1, T, stride=2), :] = odd
    hi, lo = split(tn[spot])
    tb[slot] = jnp.concatenate([hi, lo], axis=0)


def prolong(at, a_ref, base_of, row, start, pf, tb, entries, keep):
    row_of = lax.broadcasted_iota(I32, (64, 128), 0)
    row_of = jnp.where(row_of < T, 2 * row_of, 2 * row_of - 63)
    lane_of = lanes_of((64, 128))
    scale = None
    for k in range(K):
        x = stacked(raw_block(a_ref, base_of(k), row))
        rounded = x.astype(BF16).astype(F32)
        left = jnp.where(lane_of < 64, rounded, x - rounded).astype(BF16)
        keep(k, left)
        j, slot = entries(k)
        product = jnp.dot(wide(left), right_of(tb[j]), preferred_element_type=F32)
        if k == 0:
            diagonal = jnp.sum(jnp.where(row_of == lane_of, x, 0.0), axis=1, keepdims=True)
            scale = -RELAX / jnp.where(diagonal == 0.0, 1.0, diagonal)
            for pair in range(4):
                pf[at, pair] = jnp.zeros((64, 128), F32)
            value = product * scale + start
        else:
            value = product * scale
        pf[at, slot >> 1] += jnp.where(lane_of // 64 == (slot & 1), value, 0.0)


def as_right(value, nat, spot, w, e, pair):
    nat[spot, pl.ds(0, T, stride=2), :] = value[:T]
    nat[spot, pl.ds(1, T, stride=2), :] = value[T:]
    hi, lo = split(nat[spot])
    w[e, 0:64, pair * 128 : pair * 128 + 128] = hi
    w[e, 64:128, pair * 128 : pair * 128 + 128] = lo


def as_left(first, second, pt_hi, pt_lo, pair, where):
    hi, lo = split(jnp.concatenate([first, second], axis=0).T)
    pt_hi[pair * 128 : pair * 128 + 128, where] = hi
    pt_lo[pair * 128 : pair * 128 + 128, where] = lo


def place_range(counts, starts, order, batch_source, first, last, begin, dummy, unroll):
    def one(source, at):
        starts[source] = at
        after = at + ((counts[source] + QUAD - 1) >> 2)
        for q in range(QUAD):
            order[jnp.maximum(after * QUAD - QUAD, 0) + q] = dummy
        return after

    after = lax.fori_loop(first, last, one, begin)
    for q in range(QUAD * (unroll - 1)):
        order[after * QUAD + q] = dummy
    for q in range(unroll - 1):
        batch_source[after + q] = first
    return (after + unroll - 1) // unroll * unroll


def fill_order(starts, order, batch_source, rank, pair):
    source = rank >> 9
    spot = starts[source] * QUAD + (rank & 511)
    order[spot] = pair
    batch_source[spot >> 2] = source


def apply_range(order, batch_source, begin, end, lhs, w, w_from, ap, row_from, own, side, unroll):
    width = 256 if side is None else 512

    def step(i, carry):
        for u in range(unroll):
            b = i * unroll + u
            pairs = [order[b * QUAD + q] for q in range(QUAD)]
            left = wide(jnp.concatenate([lhs[pair] for pair in pairs], axis=0))
            right = right_of(w[batch_source[b] - w_from, :, :width])
            product = jnp.dot(left, right, preferred_element_type=F32)
            for q, pair in enumerate(pairs):
                e = row_from(pair >> 3)
                ap[e, own] += product[q * 64 : q * 64 + 64, :256]
                if side is not None:
                    ap[e, side] += product[q * 64 : q * 64 + 64, 256:]
        return carry

    lax.fori_loop(begin // unroll, end // unroll, step, 0)


def product3(left, right):
    (left_hi, left_lo), (right_hi, right_lo) = left, right
    return (
        jnp.dot(left_hi, right_hi, preferred_element_type=F32)
        + jnp.dot(left_hi, right_lo, preferred_element_type=F32)
        + jnp.dot(left_lo, right_hi, preferred_element_type=F32)
    )


def give(out, part, s, col, ncol, ints, mark):
    chosen = jnp.int32(0)
    place = jnp.int32(-1)
    for g in range(G):
        spot = ints[1, g].astype(I32)
        hit = lax.rem(lax.rem(spot >> 2, ncol) - col + ncol, ncol) == s
        chosen = jnp.where(hit, g, chosen)
        place = jnp.where(hit, spot & 3, place)
    low = lanes_of((T, 128)) < 64
    for pair in range(6):
        even = part[pair, pl.ds(chosen * 64, T, stride=2), :]
        odd = part[pair, pl.ds(chosen * 64 + 1, T, stride=2), :]
        first = jnp.where(low, even, pltpu.roll(odd, 64, 1))
        second = jnp.where(low, pltpu.roll(even, 64, 1), odd)
        out[2 * pair * T : (2 * pair + 1) * T, :] = first
        out[(2 * pair + 1) * T : (2 * pair + 2) * T, :] = second
    if mark:
        out[3 * G * T : 3 * G * T + 8, :] = jnp.full((8, 128), place.astype(F32))


def pack_kernel(a_own, t_own, columns, aggregate, owner, *refs, ncol):
    meta, pay_up, pay_down, pay_big, column_ints, aggregate_ints, owner_ints, sems = refs
    ints = [
        pltpu.make_async_copy(columns, column_ints, sems.at[0]),
        pltpu.make_async_copy(aggregate, aggregate_ints, sems.at[1]),
        pltpu.make_async_copy(owner, owner_ints, sems.at[2]),
    ]
    small = [
        pltpu.make_async_copy(
            t_own.at[pl.ds((R - H) * T, TH)], pay_up.at[pl.ds(0, TH)], sems.at[3]
        ),
        pltpu.make_async_copy(t_own.at[pl.ds(0, TH)], pay_down.at[pl.ds(0, TH)], sems.at[4]),
        pltpu.make_async_copy(
            t_own.at[pl.ds(0, (R - H) * T)], pay_big.at[pl.ds(K * TH, (R - H) * T)], sems.at[5]
        ),
    ]
    last = [
        pltpu.make_async_copy(
            a_own.at[pl.ds(((k + 1) * (R // H) - 1) * TH, TH)],
            pay_big.at[pl.ds(k * TH, TH)],
            sems.at[6 + k],
        )
        for k in range(K)
    ]
    for copy in ints + small + last:
        copy.start()
    meta[...] = jnp.zeros((8, 128), F32)
    for copy in ints:
        copy.wait()
    device = lax.axis_index("row") * ncol + lax.axis_index("col")
    meta[0:1, 0:R] = aggregate_ints[...].astype(F32)
    meta[1:2, 0:G] = owner_ints[...].astype(F32)
    meta[1:2, G : G + 1] = jnp.full((1, 1), device.astype(F32))
    meta[2 : 2 + K, 0:R] = column_ints[...].astype(F32)
    pay_up[TH : TH + 8, :] = meta[...]
    pay_down[TH : TH + 8, :] = meta[...]
    for copy in small + last:
        copy.wait()


def early_kernel(mine, a_own, t_in, small_up, small_down, *refs, ncol):
    ups, refs = refs[:ncol], refs[ncol:]
    part_out, ap_out, lhs_out, w_out, pt_hi_out, pt_lo_out = refs[:6]
    a_rows, tn, tb, lhs, w, pt_hi_u, pt_lo_u, pt_hi, pt_lo, ap, ap_hi, ap_lo = refs[6:18]
    part_own, part_up, t_own = refs[18:21]
    pf, nat = refs[21 : 21 + STEP], refs[21 + STEP : 21 + 2 * STEP]
    refs = refs[21 + 2 * STEP :]
    low_ints, high_ints, slots, counts, starts, ranks, order, batch_source, sems = refs
    tentative = pltpu.make_async_copy(t_in, t_own, sems.at[9])
    tentative.start()
    whole = pltpu.make_async_copy(a_own, a_rows, sems.at[2])
    whole.start()
    copies = [
        pltpu.make_async_copy(small_up.at[pl.ds(TH, 8)], low_ints, sems.at[0]),
        pltpu.make_async_copy(small_down.at[pl.ds(TH, 8)], high_ints, sems.at[1]),
    ]
    for copy in copies:
        copy.start()

    def t_rows(i, carry):
        load_tentative(t_own, (i // H) * TH, lax.rem(i, H), tn, tb, H + i)
        return carry

    def t_ends(i, carry):
        load_tentative(small_up, 0, i, tn, tb, i)
        load_tentative(small_down, 0, i, tn, tb, R + H + i)
        return carry

    lax.fori_loop(0, H, t_ends, 0, unroll=2)
    tentative.wait()
    lax.fori_loop(0, R, t_rows, 0, unroll=4)
    for copy in copies:
        copy.wait()
    device = mine[1, G].astype(I32)
    col = lax.rem(device, ncol)
    origin = device * R - H
    for i in range(H):
        slots[i] = low_ints[0, R - H + i].astype(I32) + G
        slots[H + R + i] = high_ints[0, i].astype(I32) + G
    for i in range(R):
        slots[H + i] = mine[0, i].astype(I32)
    for i in range(R + 1):
        counts[i] = 0

    lhs[R * 8] = jnp.zeros((64, 128), BF16)

    def prolong_row(i, group, u):
        row = i - group * H

        def entries(k):
            j = mine[2 + k, i].astype(I32) - origin
            source = jnp.where((j >= H) & (j < R + H), j - H, R)
            seen = counts[source]
            counts[source] = seen + 1
            ranks[i * 8 + k] = source * 512 + seen
            return j, slots[j]

        def keep(k, left):
            lhs[i * 8 + k] = left

        start = stacked(raw_block(t_own, group * TH, row))
        base_of = lambda k: (k * (R // H) + group) * TH
        prolong(i // STEP, a_rows, base_of, row, start, pf[u], tb, entries, keep)

    whole.wait()

    def prolong_rows(i, carry):
        for u in range(STEP):
            prolong_row(i * STEP + u, i // (H // STEP), u)
        return carry

    lax.fori_loop(0, R // STEP, prolong_rows, 0)

    place = lambda first, last, begin: place_range(
        counts, starts, order, batch_source, first, last, begin, R * 8, MANY
    )
    first_end = place(0, H, jnp.int32(0))
    second_end = place(H, R - H, first_end)
    third_end = place(R - H, R, second_end)
    starts[R] = MOST_EARLY

    for third in range(3):
        ap[R, third] = jnp.zeros((64, 256), F32)

    def arrange(i, carry, pairs, pt_refs, first):
        for u in range(STEP):
            e = i * STEP + u
            for pair in range(pairs):
                as_right(pf[u][i, pair], nat[u], pair, w, e, pair)
            for third in range(3):
                ap[e, third] = jnp.zeros((64, 256), F32)
            for k in range(K):
                fill_order(starts, order, batch_source, ranks[e * 8 + k], e * 8 + k)
        for u in range(0, STEP, 2):
            where = pl.ds(pl.multiple_of((i * STEP + u - first) * 64, 128), 128)
            for pair in range(pairs):
                as_left(pf[u][i, pair], pf[u + 1][i, pair], *pt_refs, pair, where)
        return carry

    inner = (pt_hi, pt_lo)
    at = [0, H // STEP, (R - H) // STEP, R // STEP]
    lax.fori_loop(at[0], at[1], lambda i, c: arrange(i, c, 4, (pt_hi_u, pt_lo_u), 0), 0)
    lax.fori_loop(at[1], at[2], lambda i, c: arrange(i, c, 2, inner, H), 0)
    lax.fori_loop(at[2], at[3], lambda i, c: arrange(i, c, 4, inner, H), 0)

    saved = [
        pltpu.make_async_copy(lhs.at[pl.ds(0, H * 8)], lhs_out, sems.at[3]),
        pltpu.make_async_copy(w.at[pl.ds(0, H)], w_out, sems.at[4]),
        pltpu.make_async_copy(pt_hi_u, pt_hi_out, sems.at[5]),
        pltpu.make_async_copy(pt_lo_u, pt_lo_out, sems.at[6]),
    ]
    for copy in saved:
        copy.start()
    same = lambda e: e
    apply_range(order, batch_source, 0, first_end, lhs, w, 0, ap, same, 1, 0, MANY)
    apply_range(order, batch_source, first_end, second_end, lhs, w, 0, ap, same, 1, None, MANY)
    apply_range(order, batch_source, second_end, third_end, lhs, w, 0, ap, same, 1, 2, MANY)

    saved.append(pltpu.make_async_copy(ap.at[pl.ds(0, H)], ap_out, sems.at[7]))
    saved[-1].start()

    def split_ap(e, carry):
        where = pl.ds(pl.multiple_of((e - H) * 64, 64), 64)
        for third in range(3):
            hi, lo = split(ap[e, third])
            ap_hi[where, third * 256 : third * 256 + 256] = hi
            ap_lo[where, third * 256 : third * 256 + 256] = lo
        return carry

    lax.fori_loop(H, R, split_ap, 0, unroll=2)

    own = product3((pt_hi[0:256, :], pt_lo[0:256, :]), (ap_hi[...], ap_lo[...]))
    for pair in range(6):
        part_own[pair] = own[:, pair * 128 : pair * 128 + 128]
    saved.append(pltpu.make_async_copy(part_own, part_out, sems.at[8]))
    saved[-1].start()
    last = slice((R - 2 * H) * 64, (R - H) * 64)
    up = product3(
        (pt_hi[256:512, last], pt_lo[256:512, last]), (ap_hi[last, :], ap_lo[last, :])
    )
    for pair in range(6):
        part_up[pair] = up[:, pair * 128 : pair * 128 + 128]
    for s in range(ncol):
        give(ups[s], part_up, s, col, ncol, high_ints, False)
    for copy in saved:
        copy.wait()


def late_kernel(mine, small_up, t_first, big, *refs, ncol):
    part_in, ap_in, lhs_in, w_in, pt_hi_in, pt_lo_in = refs[:6]
    owns, downs, refs = refs[6 : 6 + ncol], refs[6 + ncol : 6 + 2 * ncol], refs[6 + 2 * ncol :]
    tn, tb, lhs, w, pt_hi, pt_lo, ap, ap_hi, ap_lo, part_down, part_full = refs[:11]
    t_low, a_low, part_own, ap_u, lhs_u, w_u, pt_hi_u, pt_lo_u = refs[11:19]
    pf, nat = refs[19 : 19 + STEP], refs[19 + STEP : 19 + 2 * STEP]
    low_ints, slots, counts, starts, ranks, order, batch_source, sems = refs[19 + 2 * STEP :]
    copies = [
        pltpu.make_async_copy(big.at[pl.ds(K * TH, (R - H) * T)], t_low, sems.at[0]),
        pltpu.make_async_copy(small_up.at[pl.ds(TH, 8)], low_ints, sems.at[1]),
        pltpu.make_async_copy(big.at[pl.ds(0, K * TH)], a_low, sems.at[2]),
        pltpu.make_async_copy(lhs_in, lhs_u.at[pl.ds(0, H * 8)], sems.at[3]),
        pltpu.make_async_copy(w_in, w_u, sems.at[4]),
        pltpu.make_async_copy(ap_in, ap_u, sems.at[5]),
        pltpu.make_async_copy(pt_hi_in, pt_hi_u, sems.at[6]),
        pltpu.make_async_copy(pt_lo_in, pt_lo_u, sems.at[7]),
        pltpu.make_async_copy(part_in, part_own, sems.at[8]),
    ]
    for copy in copies:
        copy.start()

    def t_rows(i, carry):
        load_tentative(t_low, (i // H) * TH, lax.rem(i, H), tn, tb, i)
        return carry

    def t_ends(i, carry):
        load_tentative(small_up, 0, i, tn, tb, R - H + i)
        load_tentative(t_first, 0, i, tn, tb, R + i)
        return carry

    lax.fori_loop(0, H, t_ends, 0, unroll=2)
    copies[0].wait()
    lax.fori_loop(0, R - H, t_rows, 0, unroll=4)
    copies[1].wait()
    copies[2].wait()
    device = mine[1, G].astype(I32)
    col = lax.rem(device, ncol)
    origin = (device - 1) * R
    for i in range(R):
        slots[i] = low_ints[0, i].astype(I32) + G
    for i in range(H):
        slots[R + i] = mine[0, i].astype(I32)
    for i in range(2 * H + 1):
        counts[i] = 0

    def rank(valid, j, at):
        source = jnp.where(valid, j - (R - H), 2 * H)
        seen = counts[source]
        counts[source] = seen + 1
        ranks[at] = source * 512 + seen

    def prolong_row(i, u):
        def entries(k):
            j = low_ints[2 + k, R - H + i].astype(I32) - origin
            rank(j >= R, j, i * 8 + k)
            return j, slots[j]

        def keep(k, left):
            lhs[i * 8 + k] = left

        for k in range(K):
            j = mine[2 + k, i].astype(I32) - origin
            rank(j < R, j, (H + i) * 8 + k)
        start = stacked(raw_block(small_up, 0, i))
        prolong(i // STEP, a_low, lambda k: k * TH, i, start, pf[u], tb, entries, keep)

    def prolong_rows(i, carry):
        for u in range(STEP):
            prolong_row(i * STEP + u, u)
        return carry

    lax.fori_loop(0, H // STEP, prolong_rows, 0)

    place = lambda first, last, begin: place_range(
        counts, starts, order, batch_source, first, last, begin, H * 8, FEW
    )
    first_end = place(0, H, jnp.int32(0))
    second_end = place(H, 2 * H, first_end)
    starts[2 * H] = MOST_LATE
    lhs[H * 8] = jnp.zeros((64, 128), BF16)
    for copy in copies[3:]:
        copy.wait()
    lhs_u[H * 8] = jnp.zeros((64, 128), BF16)
    for side in range(2):
        ap[2 * H, side] = jnp.zeros((64, 256), F32)

    def arrange(i, carry):
        for u in range(STEP):
            e = i * STEP + u
            for pair in range(4):
                as_right(pf[u][i, pair], nat[u], pair, w, e, pair)
            for side in range(2):
                ap[e, side] = jnp.zeros((64, 256), F32)
                ap[H + e, side] = ap_u[e, side]
            for k in range(K):
                fill_order(starts, order, batch_source, ranks[e * 8 + k], e * 8 + k)
                fill_order(starts, order, batch_source, ranks[(H + e) * 8 + k], e * 8 + k)
        for u in range(0, STEP, 2):
            where = pl.ds(pl.multiple_of((i * STEP + u) * 64, 128), 128)
            for pair in range(4):
                as_left(pf[u][i, pair], pf[u + 1][i, pair], pt_hi, pt_lo, pair, where)
        return carry

    lax.fori_loop(0, H // STEP, arrange, 0)

    apply_range(
        order, batch_source, 0, first_end, lhs_u, w, 0, ap, lambda e: e + H, 1, 0, FEW
    )
    apply_range(
        order,
        batch_source,
        first_end,
        second_end,
        lhs,
        w_u,
        H,
        ap,
        lambda e: jnp.where(e == H, 2 * H, e),
        1,
        0,
        FEW,
    )

    def split_ap(e, carry):
        where = pl.ds(pl.multiple_of(e * 64, 64), 64)
        for side in range(2):
            hi, lo = split(ap[e, side])
            ap_hi[where, side * 256 : side * 256 + 256] = hi
            ap_lo[where, side * 256 : side * 256 + 256] = lo
        return carry

    lax.fori_loop(0, 2 * H, split_ap, 0, unroll=2)

    def split_third(e, carry):
        where = pl.ds(pl.multiple_of((H + e) * 64, 64), 64)
        hi, lo = split(ap_u[e, 2])
        ap_hi[where, 512:768] = hi
        ap_lo[where, 512:768] = lo
        return carry

    lax.fori_loop(0, H, split_third, 0, unroll=2)

    lows, highs = slice(0, H * 64), slice(H * 64, 2 * H * 64)

    def coarse(rows):
        high = product3((pt_hi_u[rows, :], pt_lo_u[rows, :]), (ap_hi[highs, :], ap_lo[highs, :]))
        low = product3((pt_hi[rows, :], pt_lo[rows, :]), (ap_hi[lows, :512], ap_lo[lows, :512]))
        return [
            high[:, pair * 128 : pair * 128 + 128]
            + (low[:, pair * 128 : pair * 128 + 128] if pair < 4 else 0.0)
            for pair in range(6)
        ]

    for pair, value in enumerate(coarse(slice(256, 512))):
        part_down[pair] = value
    for s in range(ncol):
        give(downs[s], part_down, s, col, ncol, low_ints, False)
    for pair, value in enumerate(coarse(slice(0, 256))):
        part_full[pair] = value + part_own[pair]
    for s in range(ncol):
        give(owns[s], part_full, s, col, ncol, mine, True)


MOST_EARLY = most_batches(R, R, 3, MANY)
MOST_LATE = most_batches(2 * H, 2 * H, 2, FEW)


def combine_kernel(mine, *refs, ncol):
    ups, owns, downs = refs[:ncol], refs[ncol : 2 * ncol], refs[2 * ncol : 3 * ncol]
    cross_up, cross_down, out, total = refs[3 * ncol :]
    col = lax.rem(mine[1, G].astype(I32), ncol)
    span = G * T
    for s in range(ncol):
        home = lax.rem(col - s + ncol, ncol)
        total[s, 0:span] = jnp.zeros((span, 128), F32)
        total[s, 4 * span : 5 * span] = jnp.zeros((span, 128), F32)
        total[s, span : 4 * span] = owns[s][0 : 3 * span]

        @pl.when(home > 0)
        def _():
            total[s, 0 : 3 * span] += ups[(s + 1) % ncol][...]

        @pl.when(home == 0)
        def _():
            total[s, 0 : 3 * span] += cross_up[...]

        @pl.when(home < ncol - 1)
        def _():
            total[s, 2 * span : 5 * span] += downs[(s - 1) % ncol][...]

        @pl.when(home == ncol - 1)
        def _():
            total[s, 2 * span : 5 * span] += cross_down[...]

    for j in range(G):
        for c in range(5):
            value = jnp.zeros((span, 128), F32)
            for s in range(ncol):
                mark = owns[s][3 * span : 3 * span + 1, :] == float(j)
                value = jnp.where(mark, total[s, c * span : (c + 1) * span], value)
            out[pl.ds(c * span * G + j, span, stride=G), :] = value


def local(a_blocks, columns, tentative, aggregate, owner, *, nrow, ncol):
    count = nrow * ncol
    col = lax.axis_index("col")
    up = [(d, d + 1) for d in range(count - 1)]
    down = [(d + 1, d) for d in range(count - 1)]

    def lying(blocks):
        shape = blocks.shape
        inner = blocks.reshape(*shape[:-2], shape[-2] // H, H, T, 128)
        return inner.swapaxes(-3, -2).reshape(-1, 128)

    a_own = lying(a_blocks.transpose(1, 0, 2))
    t_own = lying(tentative)
    a_own, t_own = [pltpu.with_memory_space_constraint(x, pltpu.HBM) for x in (a_own, t_own)]
    vmem = pl.BlockSpec(memory_space=pltpu.VMEM)
    smem = pl.BlockSpec(memory_space=pltpu.SMEM)
    hbm = pl.BlockSpec(memory_space=pltpu.HBM)
    meta, pay_up, pay_down, pay_big = pl.pallas_call(
        lambda *refs: pack_kernel(*refs, ncol=ncol),
        out_shape=[
            jax.ShapeDtypeStruct((8, 128), F32),
            jax.ShapeDtypeStruct((TH + 8, 128), F32),
            jax.ShapeDtypeStruct((TH + 8, 128), F32),
            jax.ShapeDtypeStruct((K * TH + (R - H) * T, 128), F32),
        ],
        in_specs=[hbm] * 5,
        out_specs=[vmem] * 4,
        scratch_shapes=[
            pltpu.VMEM((K, R), I32),
            pltpu.VMEM((1, R), I32),
            pltpu.VMEM((1, G), I32),
            pltpu.SemaphoreType.DMA((6 + K,)),
        ],
        compiler_params=pltpu.CompilerParams(vmem_limit_bytes=4 * MB),
    )(
        a_own,
        t_own,
        *[
            pltpu.with_memory_space_constraint(x, pltpu.HBM)
            for x in (columns.T, aggregate.reshape(1, R), owner.reshape(1, G))
        ],
    )
    small_up = lax.ppermute(pay_up, AXES, up)
    small_down = lax.ppermute(pay_down, AXES, down)
    big = lax.ppermute(pay_big, AXES, up)

    span = 3 * G * T
    plain = jax.ShapeDtypeStruct((span, 128), F32)
    marked = jax.ShapeDtypeStruct((span + 8, 128), F32)
    state_shapes = [
        pltpu.HBM((6, 256, 128), F32),
        pltpu.HBM((H, 3, 64, 256), F32),
        pltpu.HBM((H * 8, 64, 128), BF16),
        pltpu.HBM((H, 128, 512), BF16),
        pltpu.HBM((512, H * 64), BF16),
        pltpu.HBM((512, H * 64), BF16),
    ]
    outs = pl.pallas_call(
        lambda *refs: early_kernel(*refs, ncol=ncol),
        out_shape=[plain] * ncol + state_shapes,
        in_specs=[smem, hbm, hbm] + [vmem] * 2,
        out_specs=[vmem] * ncol + [hbm] * len(state_shapes),
        scratch_shapes=[
            pltpu.VMEM((K * R * T, 128), F32),
            pltpu.VMEM((8, 64, 128), F32),
            pltpu.VMEM((R + 2 * H, 128, 128), BF16),
            pltpu.VMEM((R * 8 + 1, 64, 128), BF16),
            pltpu.VMEM((R, 128, 512), BF16),
            pltpu.VMEM((512, H * 64), BF16),
            pltpu.VMEM((512, H * 64), BF16),
            pltpu.VMEM((512, (R - H) * 64), BF16),
            pltpu.VMEM((512, (R - H) * 64), BF16),
            pltpu.VMEM((R + 1, 3, 64, 256), F32),
            pltpu.VMEM(((R - H) * 64, 768), BF16),
            pltpu.VMEM(((R - H) * 64, 768), BF16),
            pltpu.VMEM((6, 256, 128), F32),
            pltpu.VMEM((6, 256, 128), F32),
            pltpu.VMEM((R * T, 128), F32),
            *[pltpu.VMEM((R // STEP, 4, 64, 128), F32)] * STEP,
            *[pltpu.VMEM((4, 64, 128), F32)] * STEP,
            pltpu.SMEM((8, 128), F32),
            pltpu.SMEM((8, 128), F32),
            pltpu.SMEM((R + 2 * H,), I32),
            pltpu.SMEM((R + 1,), I32),
            pltpu.SMEM((R + 1,), I32),
            pltpu.SMEM((R * 8,), I32),
            pltpu.SMEM((MOST_EARLY * QUAD + R * K,), I32),
            pltpu.SMEM((MOST_EARLY + R * K // QUAD,), I32),
            pltpu.SemaphoreType.DMA((10,)),
        ],
        compiler_params=pltpu.CompilerParams(vmem_limit_bytes=45 * MB),
        cost_estimate=pl.CostEstimate(flops=22 * 10**9, bytes_accessed=12 * MB, transcendentals=0),
    )(meta, a_own, t_own, small_up, small_down)
    ups, state = outs[:ncol], [pltpu.with_memory_space_constraint(x, pltpu.HBM) for x in outs[ncol:]]

    def rotated(blocks):
        moved = [blocks[0]]
        for s in range(1, ncol):
            route = [(c, (c + s) % ncol) for c in range(ncol)]
            moved.append(lax.ppermute(blocks[s], "col", route))
        return moved

    def chosen(blocks, index):
        value = blocks[0]
        for s in range(1, ncol):
            value = jnp.where(index == s, blocks[s], value)
        return value

    ups = rotated(ups)
    outs = pl.pallas_call(
        lambda *refs: late_kernel(*refs, ncol=ncol),
        out_shape=[marked] * ncol + [plain] * ncol,
        in_specs=[smem, vmem, vmem, hbm] + [hbm] * len(state_shapes),
        out_specs=[vmem] * (2 * ncol),
        scratch_shapes=[
            pltpu.VMEM((8, 64, 128), F32),
            pltpu.VMEM((R + H, 128, 128), BF16),
            pltpu.VMEM((H * 8 + 1, 64, 128), BF16),
            pltpu.VMEM((H, 128, 512), BF16),
            pltpu.VMEM((512, H * 64), BF16),
            pltpu.VMEM((512, H * 64), BF16),
            pltpu.VMEM((2 * H + 1, 2, 64, 256), F32),
            pltpu.VMEM((2 * H * 64, 768), BF16),
            pltpu.VMEM((2 * H * 64, 768), BF16),
            pltpu.VMEM((6, 256, 128), F32),
            pltpu.VMEM((6, 256, 128), F32),
            pltpu.VMEM(((R - H) * T, 128), F32),
            pltpu.VMEM((K * TH, 128), F32),
            pltpu.VMEM((6, 256, 128), F32),
            pltpu.VMEM((H, 3, 64, 256), F32),
            pltpu.VMEM((H * 8 + 1, 64, 128), BF16),
            pltpu.VMEM((H, 128, 512), BF16),
            pltpu.VMEM((512, H * 64), BF16),
            pltpu.VMEM((512, H * 64), BF16),
            *[pltpu.VMEM((H // STEP, 4, 64, 128), F32)] * STEP,
            *[pltpu.VMEM((4, 64, 128), F32)] * STEP,
            pltpu.SMEM((8, 128), F32),
            pltpu.SMEM((R + H,), I32),
            pltpu.SMEM((2 * H + 1,), I32),
            pltpu.SMEM((2 * H + 1,), I32),
            pltpu.SMEM((2 * H * 8,), I32),
            pltpu.SMEM((MOST_LATE * QUAD + 2 * H * K,), I32),
            pltpu.SMEM((MOST_LATE + 2 * H * K // QUAD,), I32),
            pltpu.SemaphoreType.DMA((9,)),
        ],
        compiler_params=pltpu.CompilerParams(vmem_limit_bytes=26 * MB),
    )(meta, small_up, pay_down, big, *state)
    owns, downs = outs[:ncol], outs[ncol:]
    downs = rotated(downs)
    to_next = chosen(ups, lax.rem(col + 1, ncol))
    to_last = chosen(downs, col)
    to_next, downs[0] = lax.optimization_barrier((to_next, downs[0]))
    cross_up = lax.ppermute(to_next, "row", [(r, r + 1) for r in range(nrow - 1)])
    cross_down = lax.ppermute(to_last, "row", [(r + 1, r) for r in range(nrow - 1)])
    owns = rotated(owns)
    result = pl.pallas_call(
        lambda *refs: combine_kernel(*refs, ncol=ncol),
        out_shape=jax.ShapeDtypeStruct((5 * G * T * G, 128), F32),
        in_specs=[smem] + [vmem] * (3 * ncol + 2),
        out_specs=vmem,
        scratch_shapes=[pltpu.VMEM((ncol, 5 * G * T, 128), F32)],
        compiler_params=pltpu.CompilerParams(vmem_limit_bytes=16 * MB),
    )(meta, *ups, *owns, *downs, cross_up, cross_down)
    return result.reshape(5 * G, T, G, 128).transpose(2, 0, 1, 3).reshape(G, 5 * G, T * 128)


def solution(mesh):
    placed = (
        P(AXES, None, None),
        P(AXES, None),
        P(AXES, None),
        P(AXES),
        P(AXES),
    )
    nrow, ncol = mesh.shape["row"], mesh.shape["col"]
    return jax.shard_map(
        lambda *args: local(*args, nrow=nrow, ncol=ncol),
        mesh=mesh,
        in_specs=placed,
        out_specs=P(AXES, None, None),
        check_vma=False,
    )
```

```python
import jax
import jax.numpy as jnp
from jax import lax
from jax.experimental import pallas as pl
from jax.experimental.pallas import tpu as pltpu
from jax.sharding import PartitionSpec as P

B = 64
K = 6
G = 4
R = 32
H = 8
T = 32
TH = T * H
QUAD = 4
MANY, FEW = 8, 12
STEP = 8
AXES = ("row", "col")
RELAX = 2.0 / 3.0
F32 = jnp.float32
BF16 = jnp.bfloat16
I32 = jnp.int32
MB = 1024 * 1024


def most_batches(rows, columns, ranges, unroll):
    return (rows * K + (QUAD - 1) * columns) // QUAD + ranges * (unroll - 1) + 1


def split(x):
    hi = x.astype(BF16)
    return hi, (x - hi.astype(F32)).astype(BF16)


def lanes_of(shape):
    return lax.broadcasted_iota(I32, shape, 1)


def raw_block(ref, base, row):
    return ref[pl.ds(base + row, T, stride=H), :]


def doubled(x):
    low = lanes_of((T, 128)) < 64
    other = pltpu.roll(x, 64, 1)
    return jnp.where(low, x, other), jnp.where(low, other, x)


def stacked(x):
    return jnp.concatenate(doubled(x), axis=0)


def right_of(table):
    return jnp.concatenate([table[:64], table[:64], table[64:], table[64:]], axis=0)


def wide(left):
    return jnp.concatenate([left, left], axis=1)


def load_tentative(ref, base, row, tn, tb, slot):
    even, odd = doubled(raw_block(ref, base, row))
    spot = slot & 7
    tn[spot, pl.ds(0, T, stride=2), :] = even
    tn[spot, pl.ds(1, T, stride=2), :] = odd
    hi, lo = split(tn[spot])
    tb[slot] = jnp.concatenate([hi, lo], axis=0)


def prolong(at, a_ref, base_of, row, start, pf, tb, entries, keep):
    row_of = lax.broadcasted_iota(I32, (64, 128), 0)
    row_of = jnp.where(row_of < T, 2 * row_of, 2 * row_of - 63)
    lane_of = lanes_of((64, 128))
    scale = None
    for k in range(K):
        x = stacked(raw_block(a_ref, base_of(k), row))
        rounded = x.astype(BF16).astype(F32)
        left = jnp.where(lane_of < 64, rounded, x - rounded).astype(BF16)
        keep(k, left)
        j, slot = entries(k)
        product = jnp.dot(wide(left), right_of(tb[j]), preferred_element_type=F32)
        if k == 0:
            diagonal = jnp.sum(jnp.where(row_of == lane_of, x, 0.0), axis=1, keepdims=True)
            scale = -RELAX / jnp.where(diagonal == 0.0, 1.0, diagonal)
            for pair in range(4):
                pf[at, pair] = jnp.zeros((64, 128), F32)
            value = product * scale + start
        else:
            value = product * scale
        pf[at, slot >> 1] += jnp.where(lane_of // 64 == (slot & 1), value, 0.0)


def as_right(value, nat, spot, w, e, pair):
    nat[spot, pl.ds(0, T, stride=2), :] = value[:T]
    nat[spot, pl.ds(1, T, stride=2), :] = value[T:]
    hi, lo = split(nat[spot])
    w[e, 0:64, pair * 128 : pair * 128 + 128] = hi
    w[e, 64:128, pair * 128 : pair * 128 + 128] = lo


def as_left(first, second, pt_hi, pt_lo, pair, where):
    hi, lo = split(jnp.concatenate([first, second], axis=0).T)
    pt_hi[pair * 128 : pair * 128 + 128, where] = hi
    pt_lo[pair * 128 : pair * 128 + 128, where] = lo


def place_range(counts, starts, order, batch_source, first, last, begin, dummy, unroll):
    def one(source, at):
        starts[source] = at
        after = at + ((counts[source] + QUAD - 1) >> 2)
        for q in range(QUAD):
            order[jnp.maximum(after * QUAD - QUAD, 0) + q] = dummy
        return after

    after = lax.fori_loop(first, last, one, begin)
    for q in range(QUAD * (unroll - 1)):
        order[after * QUAD + q] = dummy
    for q in range(unroll - 1):
        batch_source[after + q] = first
    return (after + unroll - 1) // unroll * unroll


def fill_order(starts, order, batch_source, rank, pair):
    source = rank >> 9
    spot = starts[source] * QUAD + (rank & 511)
    order[spot] = pair
    batch_source[spot >> 2] = source


def apply_range(order, batch_source, begin, end, lhs, w, w_from, ap, row_from, own, side, unroll):
    width = 256 if side is None else 512

    def step(i, carry):
        for u in range(unroll):
            b = i * unroll + u
            pairs = [order[b * QUAD + q] for q in range(QUAD)]
            left = wide(jnp.concatenate([lhs[pair] for pair in pairs], axis=0))
            right = right_of(w[batch_source[b] - w_from, :, :width])
            product = jnp.dot(left, right, preferred_element_type=F32)
            for q, pair in enumerate(pairs):
                e = row_from(pair >> 3)
                ap[e, own] += product[q * 64 : q * 64 + 64, :256]
                if side is not None:
                    ap[e, side] += product[q * 64 : q * 64 + 64, 256:]
        return carry

    lax.fori_loop(begin // unroll, end // unroll, step, 0)


def product3(left, right):
    (left_hi, left_lo), (right_hi, right_lo) = left, right
    return (
        jnp.dot(left_hi, right_hi, preferred_element_type=F32)
        + jnp.dot(left_hi, right_lo, preferred_element_type=F32)
        + jnp.dot(left_lo, right_hi, preferred_element_type=F32)
    )


def give(out, part, s, col, ncol, ints, mark):
    chosen = jnp.int32(0)
    place = jnp.int32(-1)
    for g in range(G):
        spot = ints[1, g].astype(I32)
        hit = lax.rem(lax.rem(spot >> 2, ncol) - col + ncol, ncol) == s
        chosen = jnp.where(hit, g, chosen)
        place = jnp.where(hit, spot & 3, place)
    low = lanes_of((T, 128)) < 64
    for pair in range(6):
        even = part[pair, pl.ds(chosen * 64, T, stride=2), :]
        odd = part[pair, pl.ds(chosen * 64 + 1, T, stride=2), :]
        first = jnp.where(low, even, pltpu.roll(odd, 64, 1))
        second = jnp.where(low, pltpu.roll(even, 64, 1), odd)
        out[2 * pair * T : (2 * pair + 1) * T, :] = first
        out[(2 * pair + 1) * T : (2 * pair + 2) * T, :] = second
    if mark:
        out[3 * G * T : 3 * G * T + 8, :] = jnp.full((8, 128), place.astype(F32))


def pack_kernel(a_own, t_own, columns, aggregate, owner, *refs, ncol):
    meta, pay_up, pay_down, pay_big, column_ints, aggregate_ints, owner_ints, sems = refs
    ints = [
        pltpu.make_async_copy(columns, column_ints, sems.at[0]),
        pltpu.make_async_copy(aggregate, aggregate_ints, sems.at[1]),
        pltpu.make_async_copy(owner, owner_ints, sems.at[2]),
    ]
    small = [
        pltpu.make_async_copy(
            t_own.at[pl.ds((R - H) * T, TH)], pay_up.at[pl.ds(0, TH)], sems.at[3]
        ),
        pltpu.make_async_copy(t_own.at[pl.ds(0, TH)], pay_down.at[pl.ds(0, TH)], sems.at[4]),
        pltpu.make_async_copy(
            t_own.at[pl.ds(0, (R - H) * T)], pay_big.at[pl.ds(K * TH, (R - H) * T)], sems.at[5]
        ),
    ]
    last = [
        pltpu.make_async_copy(
            a_own.at[pl.ds(((k + 1) * (R // H) - 1) * TH, TH)],
            pay_big.at[pl.ds(k * TH, TH)],
            sems.at[6 + k],
        )
        for k in range(K)
    ]
    for copy in ints + small + last:
        copy.start()
    meta[...] = jnp.zeros((8, 128), F32)
    for copy in ints:
        copy.wait()
    device = lax.axis_index("row") * ncol + lax.axis_index("col")
    meta[0:1, 0:R] = aggregate_ints[...].astype(F32)
    meta[1:2, 0:G] = owner_ints[...].astype(F32)
    meta[1:2, G : G + 1] = jnp.full((1, 1), device.astype(F32))
    meta[2 : 2 + K, 0:R] = column_ints[...].astype(F32)
    pay_up[TH : TH + 8, :] = meta[...]
    pay_down[TH : TH + 8, :] = meta[...]
    for copy in small + last:
        copy.wait()


def early_kernel(mine, a_own, t_in, small_up, small_down, *refs, ncol):
    ups, refs = refs[:ncol], refs[ncol:]
    part_out, ap_out, lhs_out, w_out, pt_hi_out, pt_lo_out = refs[:6]
    a_rows, tn, tb, lhs, w, pt_hi_u, pt_lo_u, pt_hi, pt_lo, ap, ap_hi, ap_lo = refs[6:18]
    part_own, part_up, t_own = refs[18:21]
    pf, nat = refs[21 : 21 + STEP], refs[21 + STEP : 21 + 2 * STEP]
    refs = refs[21 + 2 * STEP :]
    low_ints, high_ints, slots, counts, starts, ranks, order, batch_source, sems = refs
    tentative = pltpu.make_async_copy(t_in, t_own, sems.at[9])
    tentative.start()
    whole = pltpu.make_async_copy(a_own, a_rows, sems.at[2])
    whole.start()
    copies = [
        pltpu.make_async_copy(small_up.at[pl.ds(TH, 8)], low_ints, sems.at[0]),
        pltpu.make_async_copy(small_down.at[pl.ds(TH, 8)], high_ints, sems.at[1]),
    ]
    for copy in copies:
        copy.start()

    def t_rows(i, carry):
        load_tentative(t_own, (i // H) * TH, lax.rem(i, H), tn, tb, H + i)
        return carry

    def t_ends(i, carry):
        load_tentative(small_up, 0, i, tn, tb, i)
        load_tentative(small_down, 0, i, tn, tb, R + H + i)
        return carry

    lax.fori_loop(0, H, t_ends, 0, unroll=2)
    tentative.wait()
    lax.fori_loop(0, R, t_rows, 0, unroll=4)
    for copy in copies:
        copy.wait()
    device = mine[1, G].astype(I32)
    col = lax.rem(device, ncol)
    origin = device * R - H
    for i in range(H):
        slots[i] = low_ints[0, R - H + i].astype(I32) + G
        slots[H + R + i] = high_ints[0, i].astype(I32) + G
    for i in range(R):
        slots[H + i] = mine[0, i].astype(I32)
    for i in range(R + 1):
        counts[i] = 0

    lhs[R * 8] = jnp.zeros((64, 128), BF16)

    def prolong_row(i, group, u):
        row = i - group * H

        def entries(k):
            j = mine[2 + k, i].astype(I32) - origin
            source = jnp.where((j >= H) & (j < R + H), j - H, R)
            seen = counts[source]
            counts[source] = seen + 1
            ranks[i * 8 + k] = source * 512 + seen
            return j, slots[j]

        def keep(k, left):
            lhs[i * 8 + k] = left

        start = stacked(raw_block(t_own, group * TH, row))
        base_of = lambda k: (k * (R // H) + group) * TH
        prolong(i // STEP, a_rows, base_of, row, start, pf[u], tb, entries, keep)

    whole.wait()

    def prolong_rows(i, carry):
        for u in range(STEP):
            prolong_row(i * STEP + u, i // (H // STEP), u)
        return carry

    lax.fori_loop(0, R // STEP, prolong_rows, 0)

    place = lambda first, last, begin: place_range(
        counts, starts, order, batch_source, first, last, begin, R * 8, MANY
    )
    first_end = place(0, H, jnp.int32(0))
    second_end = place(H, R - H, first_end)
    third_end = place(R - H, R, second_end)
    starts[R] = MOST_EARLY

    for third in range(3):
        ap[R, third] = jnp.zeros((64, 256), F32)

    def arrange(i, carry, pairs, pt_refs, first):
        for u in range(STEP):
            e = i * STEP + u
            for pair in range(pairs):
                as_right(pf[u][i, pair], nat[u], pair, w, e, pair)
            for third in range(3):
                ap[e, third] = jnp.zeros((64, 256), F32)
            for k in range(K):
                fill_order(starts, order, batch_source, ranks[e * 8 + k], e * 8 + k)
        for u in range(0, STEP, 2):
            where = pl.ds(pl.multiple_of((i * STEP + u - first) * 64, 128), 128)
            for pair in range(pairs):
                as_left(pf[u][i, pair], pf[u + 1][i, pair], *pt_refs, pair, where)
        return carry

    inner = (pt_hi, pt_lo)
    at = [0, H // STEP, (R - H) // STEP, R // STEP]
    lax.fori_loop(at[0], at[1], lambda i, c: arrange(i, c, 4, (pt_hi_u, pt_lo_u), 0), 0)
    lax.fori_loop(at[1], at[2], lambda i, c: arrange(i, c, 2, inner, H), 0)
    lax.fori_loop(at[2], at[3], lambda i, c: arrange(i, c, 4, inner, H), 0)

    saved = [
        pltpu.make_async_copy(lhs.at[pl.ds(0, H * 8)], lhs_out, sems.at[3]),
        pltpu.make_async_copy(w.at[pl.ds(0, H)], w_out, sems.at[4]),
        pltpu.make_async_copy(pt_hi_u, pt_hi_out, sems.at[5]),
        pltpu.make_async_copy(pt_lo_u, pt_lo_out, sems.at[6]),
    ]
    for copy in saved:
        copy.start()
    same = lambda e: e
    apply_range(order, batch_source, 0, first_end, lhs, w, 0, ap, same, 1, 0, MANY)
    apply_range(order, batch_source, first_end, second_end, lhs, w, 0, ap, same, 1, None, MANY)
    apply_range(order, batch_source, second_end, third_end, lhs, w, 0, ap, same, 1, 2, MANY)

    saved.append(pltpu.make_async_copy(ap.at[pl.ds(0, H)], ap_out, sems.at[7]))
    saved[-1].start()

    def split_ap(e, carry):
        where = pl.ds(pl.multiple_of((e - H) * 64, 64), 64)
        for third in range(3):
            hi, lo = split(ap[e, third])
            ap_hi[where, third * 256 : third * 256 + 256] = hi
            ap_lo[where, third * 256 : third * 256 + 256] = lo
        return carry

    lax.fori_loop(H, R, split_ap, 0, unroll=2)

    own = product3((pt_hi[0:256, :], pt_lo[0:256, :]), (ap_hi[...], ap_lo[...]))
    for pair in range(6):
        part_own[pair] = own[:, pair * 128 : pair * 128 + 128]
    saved.append(pltpu.make_async_copy(part_own, part_out, sems.at[8]))
    saved[-1].start()
    last = slice((R - 2 * H) * 64, (R - H) * 64)
    up = product3(
        (pt_hi[256:512, last], pt_lo[256:512, last]), (ap_hi[last, :], ap_lo[last, :])
    )
    for pair in range(6):
        part_up[pair] = up[:, pair * 128 : pair * 128 + 128]
    for s in range(ncol):
        give(ups[s], part_up, s, col, ncol, high_ints, False)
    for copy in saved:
        copy.wait()


def late_kernel(mine, small_up, t_first, big, *refs, ncol):
    part_in, ap_in, lhs_in, w_in, pt_hi_in, pt_lo_in = refs[:6]
    owns, downs, refs = refs[6 : 6 + ncol], refs[6 + ncol : 6 + 2 * ncol], refs[6 + 2 * ncol :]
    tn, tb, lhs, w, pt_hi, pt_lo, ap, ap_hi, ap_lo, part_down, part_full = refs[:11]
    t_low, a_low, part_own, ap_u, lhs_u, w_u, pt_hi_u, pt_lo_u = refs[11:19]
    pf, nat = refs[19 : 19 + STEP], refs[19 + STEP : 19 + 2 * STEP]
    low_ints, slots, counts, starts, ranks, order, batch_source, sems = refs[19 + 2 * STEP :]
    copies = [
        pltpu.make_async_copy(big.at[pl.ds(K * TH, (R - H) * T)], t_low, sems.at[0]),
        pltpu.make_async_copy(small_up.at[pl.ds(TH, 8)], low_ints, sems.at[1]),
        pltpu.make_async_copy(big.at[pl.ds(0, K * TH)], a_low, sems.at[2]),
        pltpu.make_async_copy(lhs_in, lhs_u.at[pl.ds(0, H * 8)], sems.at[3]),
        pltpu.make_async_copy(w_in, w_u, sems.at[4]),
        pltpu.make_async_copy(ap_in, ap_u, sems.at[5]),
        pltpu.make_async_copy(pt_hi_in, pt_hi_u, sems.at[6]),
        pltpu.make_async_copy(pt_lo_in, pt_lo_u, sems.at[7]),
        pltpu.make_async_copy(part_in, part_own, sems.at[8]),
    ]
    for copy in copies:
        copy.start()

    def t_rows(i, carry):
        load_tentative(t_low, (i // H) * TH, lax.rem(i, H), tn, tb, i)
        return carry

    def t_ends(i, carry):
        load_tentative(small_up, 0, i, tn, tb, R - H + i)
        load_tentative(t_first, 0, i, tn, tb, R + i)
        return carry

    lax.fori_loop(0, H, t_ends, 0, unroll=2)
    copies[0].wait()
    lax.fori_loop(0, R - H, t_rows, 0, unroll=4)
    copies[1].wait()
    copies[2].wait()
    device = mine[1, G].astype(I32)
    col = lax.rem(device, ncol)
    origin = (device - 1) * R
    for i in range(R):
        slots[i] = low_ints[0, i].astype(I32) + G
    for i in range(H):
        slots[R + i] = mine[0, i].astype(I32)
    for i in range(2 * H + 1):
        counts[i] = 0

    def rank(valid, j, at):
        source = jnp.where(valid, j - (R - H), 2 * H)
        seen = counts[source]
        counts[source] = seen + 1
        ranks[at] = source * 512 + seen

    def prolong_row(i, u):
        def entries(k):
            j = low_ints[2 + k, R - H + i].astype(I32) - origin
            rank(j >= R, j, i * 8 + k)
            return j, slots[j]

        def keep(k, left):
            lhs[i * 8 + k] = left

        for k in range(K):
            j = mine[2 + k, i].astype(I32) - origin
            rank(j < R, j, (H + i) * 8 + k)
        start = stacked(raw_block(small_up, 0, i))
        prolong(i // STEP, a_low, lambda k: k * TH, i, start, pf[u], tb, entries, keep)

    def prolong_rows(i, carry):
        for u in range(STEP):
            prolong_row(i * STEP + u, u)
        return carry

    lax.fori_loop(0, H // STEP, prolong_rows, 0)

    place = lambda first, last, begin: place_range(
        counts, starts, order, batch_source, first, last, begin, H * 8, FEW
    )
    first_end = place(0, H, jnp.int32(0))
    second_end = place(H, 2 * H, first_end)
    starts[2 * H] = MOST_LATE
    lhs[H * 8] = jnp.zeros((64, 128), BF16)
    for copy in copies[3:]:
        copy.wait()
    lhs_u[H * 8] = jnp.zeros((64, 128), BF16)
    for side in range(2):
        ap[2 * H, side] = jnp.zeros((64, 256), F32)

    def arrange(i, carry):
        for u in range(STEP):
            e = i * STEP + u
            for pair in range(4):
                as_right(pf[u][i, pair], nat[u], pair, w, e, pair)
            for side in range(2):
                ap[e, side] = jnp.zeros((64, 256), F32)
                ap[H + e, side] = ap_u[e, side]
            for k in range(K):
                fill_order(starts, order, batch_source, ranks[e * 8 + k], e * 8 + k)
                fill_order(starts, order, batch_source, ranks[(H + e) * 8 + k], e * 8 + k)
        for u in range(0, STEP, 2):
            where = pl.ds(pl.multiple_of((i * STEP + u) * 64, 128), 128)
            for pair in range(4):
                as_left(pf[u][i, pair], pf[u + 1][i, pair], pt_hi, pt_lo, pair, where)
        return carry

    lax.fori_loop(0, H // STEP, arrange, 0)

    apply_range(
        order, batch_source, 0, first_end, lhs_u, w, 0, ap, lambda e: e + H, 1, 0, FEW
    )
    apply_range(
        order,
        batch_source,
        first_end,
        second_end,
        lhs,
        w_u,
        H,
        ap,
        lambda e: jnp.where(e == H, 2 * H, e),
        1,
        0,
        FEW,
    )

    def split_ap(e, carry):
        where = pl.ds(pl.multiple_of(e * 64, 64), 64)
        for side in range(2):
            hi, lo = split(ap[e, side])
            ap_hi[where, side * 256 : side * 256 + 256] = hi
            ap_lo[where, side * 256 : side * 256 + 256] = lo
        return carry

    lax.fori_loop(0, 2 * H, split_ap, 0, unroll=2)

    def split_third(e, carry):
        where = pl.ds(pl.multiple_of((H + e) * 64, 64), 64)
        hi, lo = split(ap_u[e, 2])
        ap_hi[where, 512:768] = hi
        ap_lo[where, 512:768] = lo
        return carry

    lax.fori_loop(0, H, split_third, 0, unroll=2)

    lows, highs = slice(0, H * 64), slice(H * 64, 2 * H * 64)

    def coarse(rows):
        high = product3((pt_hi_u[rows, :], pt_lo_u[rows, :]), (ap_hi[highs, :], ap_lo[highs, :]))
        low = product3((pt_hi[rows, :], pt_lo[rows, :]), (ap_hi[lows, :512], ap_lo[lows, :512]))
        return [
            high[:, pair * 128 : pair * 128 + 128]
            + (low[:, pair * 128 : pair * 128 + 128] if pair < 4 else 0.0)
            for pair in range(6)
        ]

    for pair, value in enumerate(coarse(slice(256, 512))):
        part_down[pair] = value
    for s in range(ncol):
        give(downs[s], part_down, s, col, ncol, low_ints, False)
    for pair, value in enumerate(coarse(slice(0, 256))):
        part_full[pair] = value + part_own[pair]
    for s in range(ncol):
        give(owns[s], part_full, s, col, ncol, mine, True)


MOST_EARLY = most_batches(R, R, 3, MANY)
MOST_LATE = most_batches(2 * H, 2 * H, 2, FEW)


def combine_kernel(mine, *refs, ncol):
    ups, owns, downs = refs[:ncol], refs[ncol : 2 * ncol], refs[2 * ncol : 3 * ncol]
    cross_up, cross_down, out = refs[3 * ncol :]
    col = lax.rem(mine[1, G].astype(I32), ncol)
    span = G * T
    homes = [jnp.full((span, 128), lax.rem(col - s + ncol, ncol)) for s in range(ncol)]
    for c in range(5):
        terms = []
        for s in range(ncol):
            pieces = []
            if c < 3:
                rows = slice(c * span, (c + 1) * span)
                pieces.append(
                    jnp.where(homes[s] > 0, ups[(s + 1) % ncol][rows, :], cross_up[rows, :])
                )
            if 1 <= c < 4:
                pieces.append(owns[s][(c - 1) * span : c * span, :])
            if c >= 2:
                rows = slice((c - 2) * span, (c - 1) * span)
                pieces.append(
                    jnp.where(
                        homes[s] < ncol - 1, downs[(s - 1) % ncol][rows, :], cross_down[rows, :]
                    )
                )
            terms.append(sum(pieces[1:], pieces[0]))
        for j in range(G):
            value = jnp.zeros((span, 128), F32)
            for s in range(ncol):
                mark = owns[s][3 * span : 3 * span + 1, :] == float(j)
                value = jnp.where(mark, terms[s], value)
            out[pl.ds(c * span * G + j, span, stride=G), :] = value


def local(a_blocks, columns, tentative, aggregate, owner, *, nrow, ncol):
    count = nrow * ncol
    col = lax.axis_index("col")
    up = [(d, d + 1) for d in range(count - 1)]
    down = [(d + 1, d) for d in range(count - 1)]

    def lying(blocks):
        shape = blocks.shape
        inner = blocks.reshape(*shape[:-2], shape[-2] // H, H, T, 128)
        return inner.swapaxes(-3, -2).reshape(-1, 128)

    a_own = lying(a_blocks.transpose(1, 0, 2))
    t_own = lying(tentative)
    a_own, t_own = [pltpu.with_memory_space_constraint(x, pltpu.HBM) for x in (a_own, t_own)]
    vmem = pl.BlockSpec(memory_space=pltpu.VMEM)
    smem = pl.BlockSpec(memory_space=pltpu.SMEM)
    hbm = pl.BlockSpec(memory_space=pltpu.HBM)
    meta, pay_up, pay_down, pay_big = pl.pallas_call(
        lambda *refs: pack_kernel(*refs, ncol=ncol),
        out_shape=[
            jax.ShapeDtypeStruct((8, 128), F32),
            jax.ShapeDtypeStruct((TH + 8, 128), F32),
            jax.ShapeDtypeStruct((TH + 8, 128), F32),
            jax.ShapeDtypeStruct((K * TH + (R - H) * T, 128), F32),
        ],
        in_specs=[hbm] * 5,
        out_specs=[vmem] * 4,
        scratch_shapes=[
            pltpu.VMEM((K, R), I32),
            pltpu.VMEM((1, R), I32),
            pltpu.VMEM((1, G), I32),
            pltpu.SemaphoreType.DMA((6 + K,)),
        ],
        compiler_params=pltpu.CompilerParams(vmem_limit_bytes=4 * MB),
    )(
        a_own,
        t_own,
        *[
            pltpu.with_memory_space_constraint(x, pltpu.HBM)
            for x in (columns.T, aggregate.reshape(1, R), owner.reshape(1, G))
        ],
    )
    small_up = lax.ppermute(pay_up, AXES, up)
    small_down = lax.ppermute(pay_down, AXES, down)
    big = lax.ppermute(pay_big, AXES, up)

    span = 3 * G * T
    plain = jax.ShapeDtypeStruct((span, 128), F32)
    marked = jax.ShapeDtypeStruct((span + 8, 128), F32)
    state_shapes = [
        pltpu.HBM((6, 256, 128), F32),
        pltpu.HBM((H, 3, 64, 256), F32),
        pltpu.HBM((H * 8, 64, 128), BF16),
        pltpu.HBM((H, 128, 512), BF16),
        pltpu.HBM((512, H * 64), BF16),
        pltpu.HBM((512, H * 64), BF16),
    ]
    outs = pl.pallas_call(
        lambda *refs: early_kernel(*refs, ncol=ncol),
        out_shape=[plain] * ncol + state_shapes,
        in_specs=[smem, hbm, hbm] + [vmem] * 2,
        out_specs=[vmem] * ncol + [hbm] * len(state_shapes),
        scratch_shapes=[
            pltpu.VMEM((K * R * T, 128), F32),
            pltpu.VMEM((8, 64, 128), F32),
            pltpu.VMEM((R + 2 * H, 128, 128), BF16),
            pltpu.VMEM((R * 8 + 1, 64, 128), BF16),
            pltpu.VMEM((R, 128, 512), BF16),
            pltpu.VMEM((512, H * 64), BF16),
            pltpu.VMEM((512, H * 64), BF16),
            pltpu.VMEM((512, (R - H) * 64), BF16),
            pltpu.VMEM((512, (R - H) * 64), BF16),
            pltpu.VMEM((R + 1, 3, 64, 256), F32),
            pltpu.VMEM(((R - H) * 64, 768), BF16),
            pltpu.VMEM(((R - H) * 64, 768), BF16),
            pltpu.VMEM((6, 256, 128), F32),
            pltpu.VMEM((6, 256, 128), F32),
            pltpu.VMEM((R * T, 128), F32),
            *[pltpu.VMEM((R // STEP, 4, 64, 128), F32)] * STEP,
            *[pltpu.VMEM((4, 64, 128), F32)] * STEP,
            pltpu.SMEM((8, 128), F32),
            pltpu.SMEM((8, 128), F32),
            pltpu.SMEM((R + 2 * H,), I32),
            pltpu.SMEM((R + 1,), I32),
            pltpu.SMEM((R + 1,), I32),
            pltpu.SMEM((R * 8,), I32),
            pltpu.SMEM((MOST_EARLY * QUAD + R * K,), I32),
            pltpu.SMEM((MOST_EARLY + R * K // QUAD,), I32),
            pltpu.SemaphoreType.DMA((10,)),
        ],
        compiler_params=pltpu.CompilerParams(vmem_limit_bytes=45 * MB),
        cost_estimate=pl.CostEstimate(flops=22 * 10**9, bytes_accessed=12 * MB, transcendentals=0),
    )(meta, a_own, t_own, small_up, small_down)
    ups, state = outs[:ncol], [pltpu.with_memory_space_constraint(x, pltpu.HBM) for x in outs[ncol:]]

    def rotated(blocks):
        moved = [blocks[0]]
        for s in range(1, ncol):
            route = [(c, (c + s) % ncol) for c in range(ncol)]
            moved.append(lax.ppermute(blocks[s], "col", route))
        return moved

    def chosen(blocks, index):
        value = blocks[0]
        for s in range(1, ncol):
            value = jnp.where(index == s, blocks[s], value)
        return value

    ups = rotated(ups)
    outs = pl.pallas_call(
        lambda *refs: late_kernel(*refs, ncol=ncol),
        out_shape=[marked] * ncol + [plain] * ncol,
        in_specs=[smem, vmem, vmem, hbm] + [hbm] * len(state_shapes),
        out_specs=[vmem] * (2 * ncol),
        scratch_shapes=[
            pltpu.VMEM((8, 64, 128), F32),
            pltpu.VMEM((R + H, 128, 128), BF16),
            pltpu.VMEM((H * 8 + 1, 64, 128), BF16),
            pltpu.VMEM((H, 128, 512), BF16),
            pltpu.VMEM((512, H * 64), BF16),
            pltpu.VMEM((512, H * 64), BF16),
            pltpu.VMEM((2 * H + 1, 2, 64, 256), F32),
            pltpu.VMEM((2 * H * 64, 768), BF16),
            pltpu.VMEM((2 * H * 64, 768), BF16),
            pltpu.VMEM((6, 256, 128), F32),
            pltpu.VMEM((6, 256, 128), F32),
            pltpu.VMEM(((R - H) * T, 128), F32),
            pltpu.VMEM((K * TH, 128), F32),
            pltpu.VMEM((6, 256, 128), F32),
            pltpu.VMEM((H, 3, 64, 256), F32),
            pltpu.VMEM((H * 8 + 1, 64, 128), BF16),
            pltpu.VMEM((H, 128, 512), BF16),
            pltpu.VMEM((512, H * 64), BF16),
            pltpu.VMEM((512, H * 64), BF16),
            *[pltpu.VMEM((H // STEP, 4, 64, 128), F32)] * STEP,
            *[pltpu.VMEM((4, 64, 128), F32)] * STEP,
            pltpu.SMEM((8, 128), F32),
            pltpu.SMEM((R + H,), I32),
            pltpu.SMEM((2 * H + 1,), I32),
            pltpu.SMEM((2 * H + 1,), I32),
            pltpu.SMEM((2 * H * 8,), I32),
            pltpu.SMEM((MOST_LATE * QUAD + 2 * H * K,), I32),
            pltpu.SMEM((MOST_LATE + 2 * H * K // QUAD,), I32),
            pltpu.SemaphoreType.DMA((9,)),
        ],
        compiler_params=pltpu.CompilerParams(vmem_limit_bytes=26 * MB),
    )(meta, small_up, pay_down, big, *state)
    owns, downs = outs[:ncol], outs[ncol:]
    downs = rotated(downs)
    to_next = chosen(ups, lax.rem(col + 1, ncol))
    to_last = chosen(downs, col)
    to_next, downs[0] = lax.optimization_barrier((to_next, downs[0]))
    cross_up = lax.ppermute(to_next, "row", [(r, r + 1) for r in range(nrow - 1)])
    cross_down = lax.ppermute(to_last, "row", [(r + 1, r) for r in range(nrow - 1)])
    owns = rotated(owns)
    result = pl.pallas_call(
        lambda *refs: combine_kernel(*refs, ncol=ncol),
        out_shape=jax.ShapeDtypeStruct((5 * G * T * G, 128), F32),
        in_specs=[smem] + [vmem] * (3 * ncol + 2),
        out_specs=vmem,
        compiler_params=pltpu.CompilerParams(vmem_limit_bytes=16 * MB),
    )(meta, *ups, *owns, *downs, cross_up, cross_down)
    return result.reshape(5 * G, T, G, 128).transpose(2, 0, 1, 3).reshape(G, 5 * G, T * 128)


def solution(mesh):
    placed = (
        P(AXES, None, None),
        P(AXES, None),
        P(AXES, None),
        P(AXES),
        P(AXES),
    )
    nrow, ncol = mesh.shape["row"], mesh.shape["col"]
    return jax.shard_map(
        lambda *args: local(*args, nrow=nrow, ncol=ncol),
        mesh=mesh,
        in_specs=placed,
        out_specs=P(AXES, None, None),
        check_vma=False,
    )
```
